32 devices in a mesh: rows: 32 (over z, y, x, core).
Axes of the slice: x: 2, y: 2, z: 4, core: 2. Of those that a mesh axis runs over, the one named last changes fastest.
Arguments:
- live_blocks: int32 [32], P('rows'), may hold values from 16 to 48, as said below
- tile_columns: int32 [1536, 12], P('rows'), may hold values from 0 to 143, as said below
- send_lists: int32 [32, 6, 16], P('rows'), may hold values from 0 to 47, as said below
- tiles: bfloat16 [1536, 12, 128, 128], P('rows'), may hold values from -0.09375 to 0.09375
- filter_coeffs: float32 [4], replicated, may hold values from 0.3 to 1.5
- start_block: bfloat16 [1536, 32, 128], P('rows')
- previous_block: float32 [1536, 32, 128], P('rows')
Outputs:
- basis: float32 [1536, 32, 128], P('rows')
The draws below stay inside these ranges and needn't reach their ends.
Inputs may be any that keep to these rules, and one draw needn't show every extreme that they name: `live_blocks`: at least one device has 48 live slots and one has 16. `tile_columns`: entry k = 0 of row b is b's own slot; other entries are a live own slot of the device or a ghost slot 48 + o * 16 + s. `send_lists`: every entry is below the sending device's live count.
All inputs are finite; a program needn't handle non-finite values.
Results may differ from the reference program's by a relative error of at most 0.0028.
Values may be sent and summed in bfloat16 or wider, within the bound.
A program may use at most 128 MiB of HBM per device.

```python
import math
import jax
import jax.numpy as jnp
from jax import lax

NR = 128
NV = 32
K = 12
NEIGH = 6
BD = 48
SEND = 16
NB = 1536
N_ROWS = 32


def shared_live(key):
    lowest = BD // 3
    counts = jax.random.randint(jax.random.fold_in(key, 101), (N_ROWS,), lowest, BD + 1)
    fullest = jax.random.randint(jax.random.fold_in(key, 102), (), 0, N_ROWS)
    lightest = (fullest + N_ROWS // 2) % N_ROWS
    device_ids = jnp.arange(N_ROWS)
    counts = jnp.where(device_ids == fullest, BD, counts)
    counts = jnp.where(device_ids == lightest, lowest, counts)
    return (counts.astype(jnp.int32), fullest)


def draw_live_blocks(key, part):
    return shared_live(key)[0]


def draw_tile_columns(key, part):
    counts, fullest = shared_live(key)
    block_ids = jnp.arange(NB)
    owners = block_ids // BD
    own_slot = block_ids % BD
    raw_draw = jax.random.randint(jax.random.fold_in(key, 103), (NB, K), 0, 1 << 20)
    live_here = counts[owners][:, None]
    picked = raw_draw % (live_here + NEIGH * SEND)
    columns = jnp.where(picked < live_here, picked, BD + picked - live_here)
    columns = columns.at[:, 0].set(own_slot)
    columns = columns.at[0, 1].set(BD + NEIGH * SEND - 1)
    return columns.astype(jnp.int32)


def draw_send_lists(key, part):
    counts, fullest = shared_live(key)
    raw_draw = jax.random.randint(jax.random.fold_in(key, 104), (N_ROWS, NEIGH, SEND), 0, 1 << 20)
    chosen = raw_draw % counts[:, None, None]
    chosen = chosen.at[fullest, 0, 0].set(BD - 1)
    chosen = chosen.at[fullest, 0, 1].set(0)
    return chosen.astype(jnp.int32)


def shared_field(key):
    return jax.random.normal(jax.random.fold_in(key, 201), (NB, NV, NR), jnp.float32)


def draw_start_block(key, part):
    common = shared_field(key)
    noise = jax.random.normal(jax.random.fold_in(key, 202), (NB, NV, NR), jnp.float32)
    return (common + 0.7 * noise).astype(jnp.bfloat16)


def draw_previous_block(key, part):
    common = shared_field(key)
    noise = jax.random.normal(jax.random.fold_in(key, 203), (NB, NV, NR), jnp.float32)
    return common + 0.7 * noise


def level_of(stream_key, extent, split, least, high):
    gain, own = 1.0, jax.random.fold_in(stream_key, 6)
    for position, blocks in split:
        draws = jnp.exp(jax.random.uniform(jax.random.fold_in(own, position), (blocks,), jnp.float32, least / len(split), high / len(split)))
        gain = gain * jnp.repeat(draws, extent[position] // blocks).reshape([-1 if axis == position else 1 for axis in range(len(extent))])
    return gain


def centred(own_key, dims, deviation, bound, cuts=(), held_as=jnp.bfloat16):
    gain = level_of(own_key, dims, cuts, -0.22, 0.18) if cuts else 1.0
    array = jax.random.normal(own_key, dims, jnp.float32) * deviation * gain
    return jnp.minimum(jnp.maximum(array, -bound), bound).astype(held_as)


def setup_inputs(seed: int = 0) -> dict:
    arg_keys = jax.random.split(jax.random.key(seed), 8)
    return {
        "live_blocks": draw_live_blocks(jax.random.fold_in(arg_keys[7], 71), 0),
        "tile_columns": draw_tile_columns(jax.random.fold_in(arg_keys[7], 71), 0),
        "send_lists": draw_send_lists(jax.random.fold_in(arg_keys[7], 71), 0),
        "tiles": centred(arg_keys[3], (NB, K, NR, NR), (3 * K * NR) ** -0.5, 0.09375, ((0, 32),)),
        "filter_coeffs": jnp.clip(jnp.exp(jax.random.uniform(arg_keys[4], (4,), jnp.float32, math.log(0.3), math.log(1.5))), 0.3, 1.5),
        "start_block": draw_start_block(jax.random.fold_in(arg_keys[7], 71), 0),
        "previous_block": draw_previous_block(jax.random.fold_in(arg_keys[7], 71), 0),
    }


def shift_amount(which):
    return (which // 2 + 1) * (1 if which % 2 == 0 else -1)

def gram_of(left, right):
    return jnp.einsum('bvi,bwi->vw', left, right, precision=lax.Precision.HIGHEST)

def reference(live_blocks, tile_columns, send_lists, tiles, filter_coeffs, start_block, previous_block):
    devices = N_ROWS
    block_ids = jnp.arange(NB, dtype=jnp.int32)
    retained = (block_ids % BD < live_blocks[block_ids // BD]).astype(jnp.float32)[:, None, None]
    cols_grouped = tile_columns.reshape(devices, BD, K)
    tiles_grouped = tiles.reshape(devices, BD, K, NR, NR)

    def apply_op(vectors):
        grouped = vectors.reshape(devices, BD, NV, NR)
        pieces = [grouped]
        for which in range(NEIGH):
            senders = (jnp.arange(devices, dtype=jnp.int32) - shift_amount(which)) % devices
            pieces.append(grouped[senders[:, None], send_lists[senders, which]])
        extended = jnp.concatenate(pieces, axis=1)

        def per_device(items):
            ext_dev, cols_dev, tiles_dev = items
            picked = ext_dev[cols_dev].astype(jnp.float32)
            return jnp.einsum('bkvi,bkij->bvj', picked, tiles_dev.astype(jnp.float32))
        result = lax.map(per_device, (extended, cols_grouped, tiles_grouped))
        return result.reshape(NB, NV, NR) * retained
    first_term = start_block.astype(jnp.float32) * retained
    second_term = apply_op(first_term.astype(jnp.bfloat16))
    third_term = 2.0 * apply_op(second_term.astype(jnp.bfloat16)) - first_term
    fourth_term = 2.0 * apply_op(third_term.astype(jnp.bfloat16)) - second_term
    filtered = filter_coeffs[0] * first_term + filter_coeffs[1] * second_term + filter_coeffs[2] * third_term + filter_coeffs[3] * fourth_term
    previous = previous_block * retained
    gram_prev = gram_of(previous, previous)
    cross = gram_of(previous, filtered)
    lower = jnp.linalg.cholesky(gram_prev)
    reduced = lax.linalg.triangular_solve(lower, cross, left_side=True, lower=True)
    coeff = lax.linalg.triangular_solve(lower, reduced, left_side=True, lower=True, transpose_a=True)
    cleaned = filtered - jnp.einsum('bwi,wv->bvi', previous, coeff, precision=lax.Precision.HIGHEST)
    factor = jnp.linalg.cholesky(gram_of(cleaned, cleaned))
    inverse = lax.linalg.triangular_solve(factor, jnp.eye(NV, dtype=jnp.float32), left_side=True, lower=True)
    scale = jnp.sqrt(jnp.float32(NB * NR))
    return jnp.einsum('vw,bwi->bvi', inverse, cleaned, precision=lax.Precision.HIGHEST) * scale
```

```python
import functools
import math

import jax
import jax.numpy as jnp
from jax import lax
from jax.experimental import pallas as pl
from jax.experimental.pallas import tpu as pltpu
from jax.sharding import PartitionSpec as P

MESH = pl.DeviceIdType.MESH
HIGHEST = lax.Precision.HIGHEST
GROUP = 8
PIVOTS = 8
UNROLL = 3
CHUNKS = 8
F32, BF16 = jnp.float32, jnp.bfloat16


def shift_amount(which):
    return (which // 2 + 1) * (1 if which % 2 == 0 else -1)


def iota(axis):
    return lax.broadcasted_iota(jnp.int32, (32, 128), axis)


def split(value):
    high = value.astype(BF16)
    return high, (value - high.astype(F32)).astype(BF16)


def eliminate(matrix, full):
    rows = iota(0)
    diagonal = jnp.zeros((32, 128), F32)
    for start in range(0, 32, PIVOTS):
        columns = [
            jnp.broadcast_to(matrix[:, j : j + 1], (32, 128))
            for j in range(start, start + PIVOTS)
        ]
        for p in range(PIVOTS):
            j = start + p
            row, column = matrix[j : j + 1, :], columns[p]
            keep = (rows != j) if full else (rows > j)
            factor = jnp.where(keep, column * (1.0 / column[j : j + 1, :]), 0.0)
            diagonal = jnp.where(rows == j, column, diagonal)
            matrix = matrix - factor * row
            for q in range(p + 1, PIVOTS):
                columns[q] = columns[q] - factor * columns[q][j : j + 1, :]
    return matrix, diagonal


def pack(total):
    folded = total + pltpu.roll(total, 64, 1)
    return jnp.where(iota(1)[:16] < 64, folded[:16], folded[16:])


def unpack(packed):
    return jnp.concatenate([packed, pltpu.roll(packed, 64, 1)], axis=0)


def kernel(
    n, scale, live_ref, cols_ref, sends_ref, coeff_ref, start_ref, tiles_hbm, prev_hbm, out_ref,
    tiles, prev, ext_a0, ext_b0, ext_a1, ext_b1, ext_a2, ext_b2, own_a1, own_b1, own_a2, own_b2,
    outgoing, first, accum, y_high, y_low, inverse, mine, within, across,
    tile_sem, prev_sem, halo_send, halo_recv, sum_send, sum_recv,
):
    capacity = start_ref.shape[0]
    fan = cols_ref.shape[0]
    size = capacity // CHUNKS
    neighbours, _, count = sends_ref.shape
    groups = n // GROUP
    me = lax.axis_index("rows")
    ext = [[ext_a0, ext_b0], [ext_a1, ext_b1], [ext_a2, ext_b2]]
    own = [None, [own_a1, own_b1], [own_a2, own_b2]]
    live = live_ref[0]

    prev_copy = pltpu.make_async_copy(prev_hbm, prev, prev_sem)
    prev_copy.start()
    tile_copies = []
    for c in range(CHUNKS):
        piece = pl.ds(c * size, size)
        copy = pltpu.make_async_copy(tiles_hbm.at[piece], tiles.at[piece], tile_sem.at[c])
        copy.start()
        tile_copies.append(copy)

    def halo_target(which):
        return lax.rem(me + shift_amount(which) + n, n)

    def group_mate(k):
        return me // GROUP * GROUP + lax.rem(lax.rem(me, GROUP) + k, GROUP)

    def other_group(k):
        return lax.rem(me + k * GROUP, n)

    barrier = pltpu.get_barrier_semaphore()
    partners = [halo_target(w) for w in range(neighbours)]
    partners += [group_mate(k) for k in range(1, GROUP)]
    partners += [other_group(k) for k in range(1, groups)]
    for partner in partners:
        pl.semaphore_signal(barrier, inc=1, device_id=(partner,), device_id_type=MESH)

    def gather(step, half, which):
        base = ((step * 2 + half) * neighbours + which) * count
        for s in range(count):
            index = sends_ref[which, 0, s]
            if step == 0:
                outgoing[base + s] = start_ref[index, half * 16 : half * 16 + 16]
            else:
                outgoing[base + s] = own[step][half][index]

    def halo_copy(step, half, which):
        slot = (step * 2 + half) * neighbours + which
        return pltpu.make_async_remote_copy(
            src_ref=outgoing.at[pl.ds(slot * count, count)],
            dst_ref=ext[step][half].at[pl.ds(capacity + which * count, count)],
            send_sem=halo_send.at[slot],
            recv_sem=halo_recv.at[slot],
            device_id=(halo_target(which),),
            device_id_type=MESH,
        )

    order = (4, 5, 2, 3, 0, 1)
    for half in range(2):
        for which in order:
            gather(0, half, which)
    pl.semaphore_wait(barrier, len(partners))
    for which in order:
        halo_copy(0, 0, which).start()

    def mask(b):
        return jnp.where(b < live, 1.0, 0.0).astype(F32)

    def fill(b, carry):
        value = (start_ref[b].astype(F32) * mask(b)).astype(BF16)
        ext_a0[b] = value[:16]
        ext_b0[b] = value[16:]
        return carry

    lax.fori_loop(0, capacity, fill, 0, unroll=4)

    def within_copy(which, k):
        slot = which * (GROUP - 1 + groups - 1) + k - 1
        return pltpu.make_async_remote_copy(
            src_ref=mine.at[2 * which],
            dst_ref=within.at[which * (GROUP - 1) + k - 1],
            send_sem=sum_send.at[slot],
            recv_sem=sum_recv.at[slot],
            device_id=(group_mate(k),),
            device_id_type=MESH,
        )

    def across_copy(which, k):
        slot = which * (GROUP - 1 + groups - 1) + GROUP - 1 + k - 1
        return pltpu.make_async_remote_copy(
            src_ref=mine.at[2 * which + 1],
            dst_ref=across.at[which * (groups - 1) + k - 1],
            send_sem=sum_send.at[slot],
            recv_sem=sum_recv.at[slot],
            device_id=(other_group(k),),
            device_id_type=MESH,
        )

    def sum_start(which, value):
        mine[2 * which] = value
        for k in range(1, GROUP):
            within_copy(which, k).start()

    def sum_middle(which):
        total = mine[2 * which]
        for k in range(1, GROUP):
            within_copy(which, k).wait_recv()
            total += within[which * (GROUP - 1) + k - 1]
        mine[2 * which + 1] = total
        for k in range(1, groups):
            across_copy(which, k).start()

    def sum_end(which):
        total = mine[2 * which + 1]
        for k in range(1, groups):
            across_copy(which, k).wait_recv()
            total += across[which * (groups - 1) + k - 1]
        return total

    rows_dot = functools.partial(
        lax.dot_general, dimension_numbers=(((1,), (1,)), ((), ())), preferred_element_type=F32
    )

    prev_copy.wait()

    def prev_gram(pair, total):
        left, right = [], []
        for b in (2 * pair, 2 * pair + 1):
            high, low = split(prev[b] * mask(b))
            y_high[b, :32] = high
            y_low[b, :32] = low
            left.append(jnp.concatenate([high, low], axis=0))
            right.append(jnp.concatenate([high, high, low, low], axis=0))
        return total + rows_dot(
            jnp.concatenate(left, axis=1), jnp.concatenate(right, axis=1)
        )

    total = lax.fori_loop(0, capacity // 2, prev_gram, jnp.zeros((64, 128), F32), unroll=2)
    sum_start(0, pack(total[:32] + total[32:]))
    for which in order:
        halo_copy(0, 0, which).wait_send()
    for which in order:
        halo_copy(0, 1, which).start()

    def products(step, half, b):
        vectors = ext[step][half]
        picked = [
            jnp.concatenate([vectors[cols_ref[k, row]] for k in range(fan)], axis=1)
            for row in (b, b + 1)
        ]
        result = jnp.dot(
            jnp.concatenate(picked, axis=0),
            jnp.concatenate([tiles[b], tiles[b + 1]], axis=1),
            preferred_element_type=F32,
        )
        return result[:16, :128] * mask(b), result[16:, 128:] * mask(b + 1)

    c0, c1, c2, c3 = (coeff_ref[i] for i in range(4))

    def first_step(half, b):
        for i, result in enumerate(products(0, half, b)):
            rounded = result.astype(BF16)
            first[half, b + i] = result
            own[1][half][b + i] = rounded
            ext[1][half][b + i] = rounded

    def second_step(half, b):
        for i, result in enumerate(products(1, half, b)):
            before = ext[0][half][b + i].astype(F32)
            one = first[half, b + i]
            result = 2.0 * result - before
            rounded = result.astype(BF16)
            own[2][half][b + i] = rounded
            ext[2][half][b + i] = rounded
            accum[half, b + i] = c0 * before + (c1 - c3) * one + c2 * result

    def third_step(half, b):
        rows = slice(32 + 16 * half, 48 + 16 * half)
        for i, result in enumerate(products(2, half, b)):
            high, low = split(accum[half, b + i] + (2.0 * c3) * result)
            y_high[b + i, rows] = high
            y_low[b + i, rows] = low

    def await_halo(step, half):
        for which in order:
            halo_copy(step, half, which).wait_recv()

    def loop(body, lower, upper):
        def pair(i, carry):
            body(lower + 2 * i)
            return carry

        lax.fori_loop(0, (upper - lower) // 2, pair, 0, unroll=UNROLL)

    for half in range(2):
        await_halo(0, half)
        for c in range(CHUNKS):
            if half == 0:
                tile_copies[c].wait()
                loop(functools.partial(first_step, half), c * size, (c + 1) * size)
        if half == 1:
            loop(functools.partial(first_step, half), 0, capacity)
        for which in order:
            gather(1, half, which)
            halo_copy(1, half, which).start()
        if half == 0:
            sum_middle(0)

    rows, lanes = iota(0), iota(1)
    gram = unpack(sum_end(0))
    matrix = jnp.where(lanes < 32, gram, jnp.where(lanes == rows + 64, 1.0, 0.0))
    matrix, diagonal = eliminate(matrix, True)
    middle = (lanes >= 32) & (lanes < 64)
    inverse[...] = jnp.where(middle, pltpu.roll(matrix / diagonal, 96, 1), 0.0)

    for half in range(2):
        await_halo(1, half)
        loop(functools.partial(second_step, half), 0, capacity)
        for which in order:
            gather(2, half, which)
            halo_copy(2, half, which).start()

    await_halo(2, 0)
    span = 2 * UNROLL

    def third_group(half, group):
        for i in range(UNROLL):
            third_step(half, group * span + 2 * i)

    def filtered_gram(group, total):
        for i in range(UNROLL):
            left, right = [], []
            for b in (group * span + 2 * i, group * span + 2 * i + 1):
                left.append(jnp.concatenate([y_high[b, 32:64], y_low[b, 32:64]], axis=0))
                right.append(jnp.concatenate([y_high[b], y_low[b]], axis=0))
            total += rows_dot(
                jnp.concatenate(left, axis=1), jnp.concatenate(right, axis=1)
            )
        return total

    def last_group(group, total):
        total = filtered_gram(group - 1, total)
        third_group(1, group)
        return total

    loop(functools.partial(third_step, 0), 0, capacity)
    await_halo(2, 1)
    third_group(1, 0)
    total = lax.fori_loop(1, capacity // span, last_group, jnp.zeros((64, 128), F32))
    total = filtered_gram(capacity // span - 1, total)
    sum_start(1, pack(total[:32] + total[32:]))
    sum_middle(1)
    sums = unpack(sum_end(1))

    cross = jnp.where(lanes < 32, sums, 0.0)
    below = jnp.zeros((96, 128), F32)
    coeff = jnp.dot(
        cross, jnp.concatenate([inverse[...], below], axis=0),
        precision=HIGHEST, preferred_element_type=F32,
    )
    removed = rows_dot(
        coeff, jnp.concatenate([pltpu.roll(cross, 32, 1), below], axis=0), precision=HIGHEST
    )
    matrix = jnp.where(
        lanes < 32,
        pltpu.roll(sums, 96, 1) - removed,
        jnp.where(lanes < 64, -coeff, jnp.where(lanes == rows + 64, 1.0, 0.0)),
    )
    matrix, diagonal = eliminate(matrix, False)
    factor = pltpu.roll(matrix * (scale * lax.rsqrt(diagonal)), 96, 1)
    factor = jnp.where(lanes < 64, factor, 0.0)
    high = factor.astype(BF16).astype(F32)
    both = jnp.where(lanes < 64, high, pltpu.roll(factor - high, 64, 1)).astype(BF16)
    both = jnp.concatenate([both, both], axis=1)

    def finish(pair, carry):
        stacked = []
        for b in (2 * pair, 2 * pair + 1):
            h, l = y_high[b], y_low[b]
            stacked.append(jnp.concatenate([h, h, l, l], axis=0))
        result = jnp.dot(
            both, jnp.concatenate(stacked, axis=1), preferred_element_type=F32
        )
        out_ref[2 * pair] = result[:, :128]
        out_ref[2 * pair + 1] = result[:, 128:]
        return carry

    lax.fori_loop(0, capacity // 2, finish, 0, unroll=2)

    for step in range(3):
        for half in range(2):
            for which in order:
                if (step, half) != (0, 0):
                    halo_copy(step, half, which).wait_send()
    for which in range(2):
        for k in range(1, GROUP):
            within_copy(which, k).wait_send()
        for k in range(1, groups):
            across_copy(which, k).wait_send()


def shards(
    live_blocks, tile_columns, send_lists, tiles, filter_coeffs, start_block, previous_block
):
    n = lax.axis_size("rows")
    capacity, vectors, rows = start_block.shape
    fan = tile_columns.shape[1]
    _, neighbours, count = send_lists.shape
    groups = n // GROUP
    sums = 2 * (GROUP - 1 + groups - 1)
    smem = pl.BlockSpec(memory_space=pltpu.SMEM)
    vmem = pl.BlockSpec(memory_space=pltpu.VMEM)
    hbm = pl.BlockSpec(memory_space=pl.ANY)
    half = vectors // 2
    field = pltpu.VMEM((capacity, half, rows), BF16)
    extended = pltpu.VMEM((capacity + neighbours * count, half, rows), BF16)
    wide = pltpu.VMEM((2, capacity, half, rows), F32)
    stacked = pltpu.VMEM((capacity, 2 * vectors, rows), BF16)
    scale = math.sqrt(capacity * n * rows)
    return pl.pallas_call(
        functools.partial(kernel, n, scale),
        out_shape=jax.ShapeDtypeStruct((capacity, vectors, rows), F32),
        in_specs=[smem, smem, smem, smem, vmem, hbm, hbm],
        out_specs=vmem,
        scratch_shapes=[
            pltpu.VMEM((capacity, fan * rows, rows), BF16),
            pltpu.VMEM((capacity, vectors, rows), F32),
            *[extended] * 6,
            *[field] * 4,
            pltpu.VMEM((6 * neighbours * count, half, rows), BF16),
            wide,
            wide,
            stacked,
            stacked,
            pltpu.VMEM((vectors, 128), F32),
            pltpu.VMEM((4, 16, 128), F32),
            pltpu.VMEM((2 * (GROUP - 1), 16, 128), F32),
            pltpu.VMEM((2 * (groups - 1), 16, 128), F32),
            pltpu.SemaphoreType.DMA((CHUNKS,)),
            pltpu.SemaphoreType.DMA,
            pltpu.SemaphoreType.DMA((6 * neighbours,)),
            pltpu.SemaphoreType.DMA((6 * neighbours,)),
            pltpu.SemaphoreType.DMA((sums,)),
            pltpu.SemaphoreType.DMA((sums,)),
        ],
        compiler_params=pltpu.CompilerParams(
            collective_id=0, has_side_effects=True, vmem_limit_bytes=64 * 1024 * 1024
        ),
        name="filtered_step",
    )(
        live_blocks,
        tile_columns.T,
        jnp.transpose(send_lists, (1, 0, 2)),
        filter_coeffs,
        start_block,
        tiles.reshape(capacity, fan * rows, rows),
        previous_block,
    )


def solution(mesh):
    return jax.shard_map(
        shards,
        mesh=mesh,
        in_specs=(
            P("rows"),
            P("rows", None),
            P("rows", None, None),
            P("rows", None, None, None),
            P(),
            P("rows", None, None),
            P("rows", None, None),
        ),
        out_specs=P("rows", None, None),
        check_vma=False,
    )
```

```python
import functools
import math

import jax
import jax.numpy as jnp
from jax import lax
from jax.experimental import pallas as pl
from jax.experimental.pallas import tpu as pltpu
from jax.sharding import PartitionSpec as P

MESH = pl.DeviceIdType.MESH
HIGHEST = lax.Precision.HIGHEST
GROUP = 8
PIVOTS = 8
PARTS = 4
UNROLL = 3
CHUNKS = 8
F32, BF16 = jnp.float32, jnp.bfloat16


def shift_amount(which):
    return (which // 2 + 1) * (1 if which % 2 == 0 else -1)


def iota(axis):
    return lax.broadcasted_iota(jnp.int32, (32, 128), axis)


def split(value):
    high = value.astype(BF16)
    return high, (value - high.astype(F32)).astype(BF16)


def eliminate(matrix, full):
    rows = iota(0)
    diagonal = jnp.zeros((32, 128), F32)
    for start in range(0, 32, PIVOTS):
        columns = [
            jnp.broadcast_to(matrix[:, j : j + 1], (32, 128))
            for j in range(start, start + PIVOTS)
        ]
        for p in range(PIVOTS):
            j = start + p
            row, column = matrix[j : j + 1, :], columns[p]
            keep = (rows != j) if full else (rows > j)
            factor = jnp.where(keep, column * (1.0 / column[j : j + 1, :]), 0.0)
            diagonal = jnp.where(rows == j, column, diagonal)
            matrix = matrix - factor * row
            for q in range(p + 1, PIVOTS):
                columns[q] = columns[q] - factor * columns[q][j : j + 1, :]
    return matrix, diagonal


def pack(total):
    folded = total + pltpu.roll(total, 64, 1)
    return jnp.where(iota(1)[:16] < 64, folded[:16], folded[16:])


def unpack(packed):
    return jnp.concatenate([packed, pltpu.roll(packed, 64, 1)], axis=0)


def kernel(
    n, scale, live_ref, cols_ref, sends_ref, coeff_ref, start_ref, tiles_hbm, prev_hbm,
    factor_ref, high_hbm, low_hbm,
    tiles, prev, ext_a0, ext_b0, ext_a1, ext_b1, ext_a2, ext_b2, own_a1, own_b1, own_a2, own_b2,
    outgoing, first, accum, y_high, y_low, inverse, mine, within, across,
    tile_sem, prev_sem, out_sem, halo_send, halo_recv, sum_send, sum_recv,
):
    capacity = start_ref.shape[0]
    fan = cols_ref.shape[0]
    size = capacity // CHUNKS
    neighbours, _, count = sends_ref.shape
    groups = n // GROUP
    me = lax.axis_index("rows")
    ext = [[ext_a0, ext_b0], [ext_a1, ext_b1], [ext_a2, ext_b2]]
    own = [None, [own_a1, own_b1], [own_a2, own_b2]]
    live = live_ref[0]

    prev_copy = pltpu.make_async_copy(prev_hbm, prev, prev_sem)
    prev_copy.start()
    tile_copies = []
    for c in range(CHUNKS):
        piece = pl.ds(c * size, size)
        copy = pltpu.make_async_copy(tiles_hbm.at[piece], tiles.at[piece], tile_sem.at[c])
        copy.start()
        tile_copies.append(copy)

    def halo_target(which):
        return lax.rem(me + shift_amount(which) + n, n)

    def group_mate(k):
        return me // GROUP * GROUP + lax.rem(lax.rem(me, GROUP) + k, GROUP)

    def other_group(k):
        return lax.rem(me + k * GROUP, n)

    barrier = pltpu.get_barrier_semaphore()
    partners = [halo_target(w) for w in range(neighbours)]
    partners += [group_mate(k) for k in range(1, GROUP)]
    partners += [other_group(k) for k in range(1, groups)]
    for partner in partners:
        pl.semaphore_signal(barrier, inc=1, device_id=(partner,), device_id_type=MESH)

    def gather(step, half, which):
        base = ((step * 2 + half) * neighbours + which) * count
        for s in range(count):
            index = sends_ref[which, 0, s]
            if step == 0:
                outgoing[base + s] = start_ref[index, half * 16 : half * 16 + 16]
            else:
                outgoing[base + s] = own[step][half][index]

    def halo_copy(step, half, which):
        slot = (step * 2 + half) * neighbours + which
        return pltpu.make_async_remote_copy(
            src_ref=outgoing.at[pl.ds(slot * count, count)],
            dst_ref=ext[step][half].at[pl.ds(capacity + which * count, count)],
            send_sem=halo_send.at[step * 2 + half],
            recv_sem=halo_recv.at[step * 2 + half],
            device_id=(halo_target(which),),
            device_id_type=MESH,
        )

    def halo_whole(step, half):
        ghosts = neighbours * count
        return pltpu.make_async_remote_copy(
            src_ref=outgoing.at[pl.ds((step * 2 + half) * ghosts, ghosts)],
            dst_ref=ext[step][half].at[pl.ds(capacity, ghosts)],
            send_sem=halo_send.at[step * 2 + half],
            recv_sem=halo_recv.at[step * 2 + half],
            device_id=(halo_target(0),),
            device_id_type=MESH,
        )

    order = (4, 5, 2, 3, 0, 1)
    for half in range(2):
        for which in order:
            gather(0, half, which)
    pl.semaphore_wait(barrier, len(partners))
    for which in order:
        halo_copy(0, 0, which).start()

    def mask(b):
        return jnp.where(b < live, 1.0, 0.0).astype(F32)

    def fill(b, carry):
        value = (start_ref[b].astype(F32) * mask(b)).astype(BF16)
        ext_a0[b] = value[:16]
        ext_b0[b] = value[16:]
        return carry

    lax.fori_loop(0, capacity, fill, 0, unroll=4)

    def within_copy(which, k):
        return pltpu.make_async_remote_copy(
            src_ref=mine.at[2 * which],
            dst_ref=within.at[which * (GROUP - 1) + k - 1],
            send_sem=sum_send.at[2 * which],
            recv_sem=sum_recv.at[2 * which],
            device_id=(group_mate(k),),
            device_id_type=MESH,
        )

    def across_copy(which, k):
        return pltpu.make_async_remote_copy(
            src_ref=mine.at[2 * which + 1],
            dst_ref=across.at[which * (groups - 1) + k - 1],
            send_sem=sum_send.at[2 * which + 1],
            recv_sem=sum_recv.at[2 * which + 1],
            device_id=(other_group(k),),
            device_id_type=MESH,
        )

    def sum_whole(which, landing):
        peers = landing.shape[0] // 2
        slot = 2 * which + (0 if landing is within else 1)
        return pltpu.make_async_remote_copy(
            src_ref=landing.at[pl.ds(which * peers, peers)],
            dst_ref=landing.at[pl.ds(which * peers, peers)],
            send_sem=sum_send.at[slot],
            recv_sem=sum_recv.at[slot],
            device_id=(group_mate(1),),
            device_id_type=MESH,
        )

    def sum_start(which, value):
        mine[2 * which] = value
        for k in range(1, GROUP):
            within_copy(which, k).start()

    def sum_middle(which):
        total = mine[2 * which]
        sum_whole(which, within).wait_recv()
        for k in range(1, GROUP):
            total += within[which * (GROUP - 1) + k - 1]
        mine[2 * which + 1] = total
        for k in range(1, groups):
            across_copy(which, k).start()

    def sum_end(which):
        total = mine[2 * which + 1]
        sum_whole(which, across).wait_recv()
        for k in range(1, groups):
            total += across[which * (groups - 1) + k - 1]
        return total

    rows_dot = functools.partial(
        lax.dot_general, dimension_numbers=(((1,), (1,)), ((), ())), preferred_element_type=F32
    )

    prev_copy.wait()

    def prev_gram(pair, total):
        left, right = [], []
        for b in (2 * pair, 2 * pair + 1):
            high, low = split(prev[b] * mask(b))
            y_high[b, :32] = high
            y_low[b, :32] = low
            left.append(jnp.concatenate([high, low], axis=0))
            right.append(jnp.concatenate([high, high, low, low], axis=0))
        return total + rows_dot(
            jnp.concatenate(left, axis=1), jnp.concatenate(right, axis=1)
        )

    total = lax.fori_loop(0, capacity // 2, prev_gram, jnp.zeros((64, 128), F32), unroll=2)
    sum_start(0, pack(total[:32] + total[32:]))
    halo_whole(0, 0).wait_send()
    for which in order:
        halo_copy(0, 1, which).start()

    def products(step, half, b):
        vectors = ext[step][half]
        picked = [
            jnp.concatenate([vectors[cols_ref[k, row]] for k in range(fan)], axis=1)
            for row in (b, b + 1)
        ]
        result = jnp.dot(
            jnp.concatenate(picked, axis=0),
            jnp.concatenate([tiles[b], tiles[b + 1]], axis=1),
            preferred_element_type=F32,
        )
        return result[:16, :128] * mask(b), result[16:, 128:] * mask(b + 1)

    c0, c1, c2, c3 = (coeff_ref[i] for i in range(4))

    def first_step(half, b):
        for i, result in enumerate(products(0, half, b)):
            rounded = result.astype(BF16)
            first[half, b + i] = result
            own[1][half][b + i] = rounded
            ext[1][half][b + i] = rounded

    def second_step(half, b):
        for i, result in enumerate(products(1, half, b)):
            before = ext[0][half][b + i].astype(F32)
            one = first[half, b + i]
            result = 2.0 * result - before
            rounded = result.astype(BF16)
            own[2][half][b + i] = rounded
            ext[2][half][b + i] = rounded
            accum[half, b + i] = c0 * before + (c1 - c3) * one + c2 * result

    def third_step(half, b):
        rows = slice(32 + 16 * half, 48 + 16 * half)
        for i, result in enumerate(products(2, half, b)):
            high, low = split(accum[half, b + i] + (2.0 * c3) * result)
            y_high[b + i, rows] = high
            y_low[b + i, rows] = low

    def await_halo(step, half):
        halo_whole(step, half).wait_recv()

    def loop(body, lower, upper):
        def pair(i, carry):
            body(lower + 2 * i)
            return carry

        lax.fori_loop(0, (upper - lower) // 2, pair, 0, unroll=UNROLL)

    for half in range(2):
        await_halo(0, half)
        for c in range(CHUNKS):
            if half == 0:
                tile_copies[c].wait()
                loop(functools.partial(first_step, half), c * size, (c + 1) * size)
        if half == 1:
            loop(functools.partial(first_step, half), 0, capacity)
        for which in order:
            gather(1, half, which)
            halo_copy(1, half, which).start()
        if half == 0:
            sum_middle(0)

    rows, lanes = iota(0), iota(1)
    gram = unpack(sum_end(0))
    matrix = jnp.where(lanes < 32, gram, jnp.where(lanes == rows + 64, 1.0, 0.0))
    matrix, diagonal = eliminate(matrix, True)
    middle = (lanes >= 32) & (lanes < 64)
    inverse[...] = jnp.where(middle, pltpu.roll(matrix / diagonal, 96, 1), 0.0)

    for half in range(2):
        await_halo(1, half)
        loop(functools.partial(second_step, half), 0, capacity)
        for which in order:
            gather(2, half, which)
            halo_copy(2, half, which).start()

    await_halo(2, 0)
    span = 2 * UNROLL

    def third_group(half, group):
        for i in range(UNROLL):
            third_step(half, group * span + 2 * i)

    def filtered_gram(group, total):
        for i in range(UNROLL):
            left, right = [], []
            for b in (group * span + 2 * i, group * span + 2 * i + 1):
                left.append(jnp.concatenate([y_high[b, 32:64], y_low[b, 32:64]], axis=0))
                right.append(jnp.concatenate([y_high[b], y_low[b]], axis=0))
            total += rows_dot(
                jnp.concatenate(left, axis=1), jnp.concatenate(right, axis=1)
            )
        return total

    def last_group(group, total):
        total = filtered_gram(group - 1, total)
        third_group(1, group)
        return total

    loop(functools.partial(third_step, 0), 0, capacity)
    await_halo(2, 1)
    third_group(1, 0)
    total = lax.fori_loop(1, capacity // span, last_group, jnp.zeros((64, 128), F32))
    total = filtered_gram(capacity // span - 1, total)
    out_copies = [
        pltpu.make_async_copy(y_high, high_hbm, out_sem.at[0]),
        pltpu.make_async_copy(y_low, low_hbm, out_sem.at[1]),
    ]
    sum_start(1, pack(total[:32] + total[32:]))
    for copy in out_copies:
        copy.start()
    sum_middle(1)
    sums = unpack(sum_end(1))

    cross = jnp.where(lanes < 32, sums, 0.0)
    below = jnp.zeros((96, 128), F32)
    coeff = jnp.dot(
        cross, jnp.concatenate([inverse[...], below], axis=0),
        precision=HIGHEST, preferred_element_type=F32,
    )
    removed = rows_dot(
        coeff, jnp.concatenate([pltpu.roll(cross, 32, 1), below], axis=0), precision=HIGHEST
    )
    matrix = jnp.where(
        lanes < 32,
        pltpu.roll(sums, 96, 1) - removed,
        jnp.where(lanes < 64, -coeff, jnp.where(lanes == rows + 64, 1.0, 0.0)),
    )
    matrix, diagonal = eliminate(matrix, False)
    factor = pltpu.roll(matrix * (scale * lax.rsqrt(diagonal)), 96, 1)
    factor = jnp.where(lanes < 64, factor, 0.0)
    high = factor.astype(BF16).astype(F32)
    both = jnp.where(lanes < 64, high, pltpu.roll(factor - high, 64, 1)).astype(BF16)
    factor_ref[...] = jnp.concatenate([both, both], axis=1)

    def finish(pair, carry):
        stacked = []
        for b in (2 * pair, 2 * pair + 1):
            h, l = y_high[b], y_low[b]
            stacked.append(jnp.concatenate([h, h, l, l], axis=0))
        result = jnp.dot(
            both, jnp.concatenate(stacked, axis=1), preferred_element_type=F32
        )
        out_ref[2 * pair] = result[:, :128]
        out_ref[2 * pair + 1] = result[:, 128:]
        return carry

    for copy in out_copies:
        copy.wait()
    for step in range(3):
        for half in range(2):
            if (step, half) != (0, 0):
                halo_whole(step, half).wait_send()
    for which in range(2):
        sum_whole(which, within).wait_send()
        sum_whole(which, across).wait_send()


def finish(
    factor_hbm, high_hbm, low_hbm, out_hbm, factor_ref, high, low, out,
    factor_sem, in_sem, out_sem,
):
    size = high.shape[0] // PARTS
    pieces = [pl.ds(c * size, size) for c in range(PARTS)]
    reads = [
        [
            pltpu.make_async_copy(high_hbm.at[piece], high.at[piece], in_sem.at[0, c]),
            pltpu.make_async_copy(low_hbm.at[piece], low.at[piece], in_sem.at[1, c]),
        ]
        for c, piece in enumerate(pieces)
    ]
    writes = [
        pltpu.make_async_copy(out.at[piece], out_hbm.at[piece], out_sem.at[c])
        for c, piece in enumerate(pieces)
    ]
    factor_copy = pltpu.make_async_copy(factor_hbm, factor_ref, factor_sem)
    factor_copy.start()
    for pair in reads:
        for copy in pair:
            copy.start()
    factor_copy.wait()
    factor = factor_ref[...]
    for c in range(PARTS):
        for copy in reads[c]:
            copy.wait()
        for b in range(c * size, (c + 1) * size, 2):
            stacked = [
                jnp.concatenate([high[i], high[i], low[i], low[i]], axis=0) for i in (b, b + 1)
            ]
            result = jnp.dot(
                factor, jnp.concatenate(stacked, axis=1), preferred_element_type=F32
            )
            out[b] = result[:, :128]
            out[b + 1] = result[:, 128:]
        writes[c].start()
    for copy in writes:
        copy.wait()


def shards(
    live_blocks, tile_columns, send_lists, tiles, filter_coeffs, start_block, previous_block
):
    n = lax.axis_size("rows")
    capacity, vectors, rows = start_block.shape
    fan = tile_columns.shape[1]
    _, neighbours, count = send_lists.shape
    groups = n // GROUP
    smem = pl.BlockSpec(memory_space=pltpu.SMEM)
    vmem = pl.BlockSpec(memory_space=pltpu.VMEM)
    hbm = pl.BlockSpec(memory_space=pl.ANY)
    half = vectors // 2
    field = pltpu.VMEM((capacity, half, rows), BF16)
    extended = pltpu.VMEM((capacity + neighbours * count, half, rows), BF16)
    wide = pltpu.VMEM((2, capacity, half, rows), F32)
    stacked = pltpu.VMEM((capacity, 2 * vectors, rows), BF16)
    scale = math.sqrt(capacity * n * rows)
    factor, high, low = pl.pallas_call(
        functools.partial(kernel, n, scale),
        out_shape=[jax.ShapeDtypeStruct((vectors, 256), BF16)]
        + [jax.ShapeDtypeStruct((capacity, 2 * vectors, rows), BF16)] * 2,
        in_specs=[smem, smem, smem, smem, vmem, hbm, hbm],
        out_specs=[vmem, hbm, hbm],
        scratch_shapes=[
            pltpu.VMEM((capacity, fan * rows, rows), BF16),
            pltpu.VMEM((capacity, vectors, rows), F32),
            *[extended] * 6,
            *[field] * 4,
            pltpu.VMEM((6 * neighbours * count, half, rows), BF16),
            wide,
            wide,
            stacked,
            stacked,
            pltpu.VMEM((vectors, 128), F32),
            pltpu.VMEM((4, 16, 128), F32),
            pltpu.VMEM((2 * (GROUP - 1), 16, 128), F32),
            pltpu.VMEM((2 * (groups - 1), 16, 128), F32),
            pltpu.SemaphoreType.DMA((CHUNKS,)),
            pltpu.SemaphoreType.DMA,
            pltpu.SemaphoreType.DMA((2,)),
            pltpu.SemaphoreType.DMA((6,)),
            pltpu.SemaphoreType.DMA((6,)),
            pltpu.SemaphoreType.DMA((4,)),
            pltpu.SemaphoreType.DMA((4,)),
        ],
        compiler_params=pltpu.CompilerParams(
            collective_id=0, has_side_effects=True, vmem_limit_bytes=64 * 1024 * 1024
        ),
        name="filtered_step",
    )(
        live_blocks,
        tile_columns.T,
        jnp.transpose(send_lists, (1, 0, 2)),
        filter_coeffs,
        start_block,
        tiles.reshape(capacity, fan * rows, rows),
        previous_block,
    )
    return pl.pallas_call(
        finish,
        out_shape=jax.ShapeDtypeStruct((capacity, vectors, rows), F32),
        in_specs=[hbm, hbm, hbm],
        out_specs=hbm,
        scratch_shapes=[
            pltpu.VMEM((vectors, 256), BF16),
            stacked,
            stacked,
            pltpu.VMEM((capacity, vectors, rows), F32),
            pltpu.SemaphoreType.DMA,
            pltpu.SemaphoreType.DMA((2, PARTS)),
            pltpu.SemaphoreType.DMA((PARTS,)),
        ],
        compiler_params=pltpu.CompilerParams(vmem_limit_bytes=64 * 1024 * 1024),
        name="finish",
    )(factor, high, low)


def solution(mesh):
    return jax.shard_map(
        shards,
        mesh=mesh,
        in_specs=(
            P("rows"),
            P("rows", None),
            P("rows", None, None),
            P("rows", None, None, None),
            P(),
            P("rows", None, None),
            P("rows", None, None),
        ),
        out_specs=P("rows", None, None),
        check_vma=False,
    )
```

```python
import functools
import math

import jax
import jax.numpy as jnp
from jax import lax
from jax.experimental import pallas as pl
from jax.experimental.pallas import tpu as pltpu
from jax.sharding import PartitionSpec as P

MESH = pl.DeviceIdType.MESH
HIGHEST = lax.Precision.HIGHEST
GROUP = 8
PIVOTS = 8
PARTS = 4
UNROLL = 3
CHUNKS = 8
F32, BF16 = jnp.float32, jnp.bfloat16


def shift_amount(which):
    return (which // 2 + 1) * (1 if which % 2 == 0 else -1)


def iota(axis):
    return lax.broadcasted_iota(jnp.int32, (32, 128), axis)


def split(value):
    high = value.astype(BF16)
    return high, (value - high.astype(F32)).astype(BF16)


def eliminate(matrix, full):
    rows = iota(0)
    diagonal = jnp.zeros((32, 128), F32)
    for start in range(0, 32, PIVOTS):
        columns = [
            jnp.broadcast_to(matrix[:, j : j + 1], (32, 128))
            for j in range(start, start + PIVOTS)
        ]
        for p in range(PIVOTS):
            j = start + p
            row, column = matrix[j : j + 1, :], columns[p]
            keep = (rows != j) if full else (rows > j)
            factor = jnp.where(keep, column * (1.0 / column[j : j + 1, :]), 0.0)
            diagonal = jnp.where(rows == j, column, diagonal)
            matrix = matrix - factor * row
            for q in range(p + 1, PIVOTS):
                columns[q] = columns[q] - factor * columns[q][j : j + 1, :]
    return matrix, diagonal


def pack(total):
    folded = total + pltpu.roll(total, 64, 1)
    return jnp.where(iota(1)[:16] < 64, folded[:16], folded[16:])


def unpack(packed):
    return jnp.concatenate([packed, pltpu.roll(packed, 64, 1)], axis=0)


def kernel(
    n, scale, live_hbm, cols_hbm, sends_hbm, coeff_hbm, start_hbm, tiles_hbm, prev_hbm,
    factor_ref, high_hbm, low_hbm,
    live_ref, cols_ref, sends_ref, coeff_ref, start_ref, tiles, prev, ext_a0, ext_b0, ext_a1, ext_b1, ext_a2, ext_b2, own_a1, own_b1, own_a2, own_b2,
    outgoing, first, accum, y_high, y_low, inverse, mine, within, across,
    entry_sem, tile_sem, prev_sem, out_sem, halo_send, halo_recv, sum_send, sum_recv,
):
    capacity = start_ref.shape[0]
    fan = cols_ref.shape[0]
    size = capacity // CHUNKS
    neighbours, _, count = sends_ref.shape
    groups = n // GROUP
    me = lax.axis_index("rows")
    ext = [[ext_a0, ext_b0], [ext_a1, ext_b1], [ext_a2, ext_b2]]
    own = [None, [own_a1, own_b1], [own_a2, own_b2]]
    def halo_target(which):
        return lax.rem(me + shift_amount(which) + n, n)

    def group_mate(k):
        return me // GROUP * GROUP + lax.rem(lax.rem(me, GROUP) + k, GROUP)

    def other_group(k):
        return lax.rem(me + k * GROUP, n)

    barrier = pltpu.get_barrier_semaphore()
    partners = [halo_target(w) for w in range(neighbours)]
    partners += [group_mate(k) for k in range(1, GROUP)]
    partners += [other_group(k) for k in range(1, groups)]
    for partner in partners:
        pl.semaphore_signal(barrier, inc=1, device_id=(partner,), device_id_type=MESH)

    def entry_copy(source, target, which):
        return pltpu.make_async_copy(source, target, entry_sem.at[which])

    entries = [
        entry_copy(*pair, i)
        for i, pair in enumerate(
            [
                (sends_hbm, sends_ref),
                (start_hbm, start_ref),
                (live_hbm, live_ref),
                (cols_hbm, cols_ref),
                (coeff_hbm, coeff_ref),
            ]
        )
    ]
    prev_copy = pltpu.make_async_copy(prev_hbm, prev, prev_sem)
    tile_copies = []
    for c in range(CHUNKS):
        piece = pl.ds(c * size, size)
        tile_copies.append(
            pltpu.make_async_copy(tiles_hbm.at[piece], tiles.at[piece], tile_sem.at[c])
        )
    for copy in entries:
        copy.start()
    prev_copy.start()
    tile_copies[0].start()

    def gather(step, half, which):
        base = ((step * 2 + half) * neighbours + which) * count
        for s in range(count):
            index = sends_ref[which, 0, s]
            if step == 0:
                outgoing[base + s] = start_ref[index, half * 16 : half * 16 + 16]
            else:
                outgoing[base + s] = own[step][half][index]

    def halo_copy(step, half, which):
        slot = (step * 2 + half) * neighbours + which
        return pltpu.make_async_remote_copy(
            src_ref=outgoing.at[pl.ds(slot * count, count)],
            dst_ref=ext[step][half].at[pl.ds(capacity + which * count, count)],
            send_sem=halo_send.at[step * 2 + half],
            recv_sem=halo_recv.at[step * 2 + half],
            device_id=(halo_target(which),),
            device_id_type=MESH,
        )

    def halo_whole(step, half):
        ghosts = neighbours * count
        return pltpu.make_async_remote_copy(
            src_ref=outgoing.at[pl.ds((step * 2 + half) * ghosts, ghosts)],
            dst_ref=ext[step][half].at[pl.ds(capacity, ghosts)],
            send_sem=halo_send.at[step * 2 + half],
            recv_sem=halo_recv.at[step * 2 + half],
            device_id=(halo_target(0),),
            device_id_type=MESH,
        )

    order = (4, 5, 2, 3, 0, 1)
    entries[0].wait()
    entries[1].wait()
    for half in range(2):
        for which in order:
            gather(0, half, which)
    pl.semaphore_wait(barrier, len(partners))
    for which in order:
        halo_copy(0, 0, which).start()

    for copy in entries[2:]:
        copy.wait()
    live = live_ref[0]

    def mask(b):
        return jnp.where(b < live, 1.0, 0.0).astype(F32)

    def fill(b, carry):
        value = (start_ref[b].astype(F32) * mask(b)).astype(BF16)
        ext_a0[b] = value[:16]
        ext_b0[b] = value[16:]
        return carry

    lax.fori_loop(0, capacity, fill, 0, unroll=4)

    def within_copy(which, k):
        return pltpu.make_async_remote_copy(
            src_ref=mine.at[2 * which],
            dst_ref=within.at[which * (GROUP - 1) + k - 1],
            send_sem=sum_send.at[2 * which],
            recv_sem=sum_recv.at[2 * which],
            device_id=(group_mate(k),),
            device_id_type=MESH,
        )

    def across_copy(which, k):
        return pltpu.make_async_remote_copy(
            src_ref=mine.at[2 * which + 1],
            dst_ref=across.at[which * (groups - 1) + k - 1],
            send_sem=sum_send.at[2 * which + 1],
            recv_sem=sum_recv.at[2 * which + 1],
            device_id=(other_group(k),),
            device_id_type=MESH,
        )

    def sum_whole(which, landing):
        peers = landing.shape[0] // 2
        slot = 2 * which + (0 if landing is within else 1)
        return pltpu.make_async_remote_copy(
            src_ref=landing.at[pl.ds(which * peers, peers)],
            dst_ref=landing.at[pl.ds(which * peers, peers)],
            send_sem=sum_send.at[slot],
            recv_sem=sum_recv.at[slot],
            device_id=(group_mate(1),),
            device_id_type=MESH,
        )

    def sum_start(which, value):
        mine[2 * which] = value
        for k in range(1, GROUP):
            within_copy(which, k).start()

    def sum_middle(which):
        total = mine[2 * which]
        sum_whole(which, within).wait_recv()
        for k in range(1, GROUP):
            total += within[which * (GROUP - 1) + k - 1]
        mine[2 * which + 1] = total
        for k in range(1, groups):
            across_copy(which, k).start()

    def sum_end(which):
        total = mine[2 * which + 1]
        sum_whole(which, across).wait_recv()
        for k in range(1, groups):
            total += across[which * (groups - 1) + k - 1]
        return total

    rows_dot = functools.partial(
        lax.dot_general, dimension_numbers=(((1,), (1,)), ((), ())), preferred_element_type=F32
    )

    prev_copy.wait()
    for copy in tile_copies[1:]:
        copy.start()

    def prev_gram(pair, total):
        left, right = [], []
        for b in (2 * pair, 2 * pair + 1):
            high, low = split(prev[b] * mask(b))
            y_high[b, :32] = high
            y_low[b, :32] = low
            left.append(jnp.concatenate([high, low], axis=0))
            right.append(jnp.concatenate([high, high, low, low], axis=0))
        return total + rows_dot(
            jnp.concatenate(left, axis=1), jnp.concatenate(right, axis=1)
        )

    total = lax.fori_loop(0, capacity // 2, prev_gram, jnp.zeros((64, 128), F32), unroll=2)
    sum_start(0, pack(total[:32] + total[32:]))
    halo_whole(0, 0).wait_send()
    for which in order:
        halo_copy(0, 1, which).start()

    def products(step, half, b):
        vectors = ext[step][half]
        picked = [
            jnp.concatenate([vectors[cols_ref[k, row]] for k in range(fan)], axis=1)
            for row in (b, b + 1)
        ]
        result = jnp.dot(
            jnp.concatenate(picked, axis=0),
            jnp.concatenate([tiles[b], tiles[b + 1]], axis=1),
            preferred_element_type=F32,
        )
        return result[:16, :128] * mask(b), result[16:, 128:] * mask(b + 1)

    c0, c1, c2, c3 = (coeff_ref[i] for i in range(4))

    def first_step(half, b):
        for i, result in enumerate(products(0, half, b)):
            rounded = result.astype(BF16)
            first[half, b + i] = result
            own[1][half][b + i] = rounded
            ext[1][half][b + i] = rounded

    def second_step(half, b):
        for i, result in enumerate(products(1, half, b)):
            before = ext[0][half][b + i].astype(F32)
            one = first[half, b + i]
            result = 2.0 * result - before
            rounded = result.astype(BF16)
            own[2][half][b + i] = rounded
            ext[2][half][b + i] = rounded
            accum[half, b + i] = c0 * before + (c1 - c3) * one + c2 * result

    def third_step(half, b):
        rows = slice(32 + 16 * half, 48 + 16 * half)
        for i, result in enumerate(products(2, half, b)):
            high, low = split(accum[half, b + i] + (2.0 * c3) * result)
            y_high[b + i, rows] = high
            y_low[b + i, rows] = low

    def await_halo(step, half):
        halo_whole(step, half).wait_recv()

    def loop(body, lower, upper):
        def pair(i, carry):
            body(lower + 2 * i)
            return carry

        lax.fori_loop(0, (upper - lower) // 2, pair, 0, unroll=UNROLL)

    for half in range(2):
        await_halo(0, half)
        for c in range(CHUNKS):
            if half == 0:
                tile_copies[c].wait()
                loop(functools.partial(first_step, half), c * size, (c + 1) * size)
        if half == 1:
            loop(functools.partial(first_step, half), 0, capacity)
        for which in order:
            gather(1, half, which)
            halo_copy(1, half, which).start()
        if half == 0:
            sum_middle(0)

    rows, lanes = iota(0), iota(1)
    gram = unpack(sum_end(0))
    matrix = jnp.where(lanes < 32, gram, jnp.where(lanes == rows + 64, 1.0, 0.0))
    matrix, diagonal = eliminate(matrix, True)
    middle = (lanes >= 32) & (lanes < 64)
    inverse[...] = jnp.where(middle, pltpu.roll(matrix / diagonal, 96, 1), 0.0)

    for half in range(2):
        await_halo(1, half)
        loop(functools.partial(second_step, half), 0, capacity)
        for which in order:
            gather(2, half, which)
            halo_copy(2, half, which).start()

    await_halo(2, 0)
    span = 2 * UNROLL

    def third_group(half, group):
        for i in range(UNROLL):
            third_step(half, group * span + 2 * i)

    def filtered_gram(group, total):
        for i in range(UNROLL):
            left, right = [], []
            for b in (group * span + 2 * i, group * span + 2 * i + 1):
                left.append(jnp.concatenate([y_high[b, 32:64], y_low[b, 32:64]], axis=0))
                right.append(jnp.concatenate([y_high[b], y_low[b]], axis=0))
            total += rows_dot(
                jnp.concatenate(left, axis=1), jnp.concatenate(right, axis=1)
            )
        return total

    def last_group(group, total):
        total = filtered_gram(group - 1, total)
        third_group(1, group)
        return total

    loop(functools.partial(third_step, 0), 0, capacity)
    await_halo(2, 1)
    third_group(1, 0)
    total = lax.fori_loop(1, capacity // span, last_group, jnp.zeros((64, 128), F32))
    total = filtered_gram(capacity // span - 1, total)
    out_copies = [
        pltpu.make_async_copy(y_high, high_hbm, out_sem.at[0]),
        pltpu.make_async_copy(y_low, low_hbm, out_sem.at[1]),
    ]
    sum_start(1, pack(total[:32] + total[32:]))
    for copy in out_copies:
        copy.start()
    sum_middle(1)
    sums = unpack(sum_end(1))

    cross = jnp.where(lanes < 32, sums, 0.0)
    below = jnp.zeros((96, 128), F32)
    coeff = jnp.dot(
        cross, jnp.concatenate([inverse[...], below], axis=0),
        precision=HIGHEST, preferred_element_type=F32,
    )
    removed = rows_dot(
        coeff, jnp.concatenate([pltpu.roll(cross, 32, 1), below], axis=0), precision=HIGHEST
    )
    matrix = jnp.where(
        lanes < 32,
        pltpu.roll(sums, 96, 1) - removed,
        jnp.where(lanes < 64, -coeff, jnp.where(lanes == rows + 64, 1.0, 0.0)),
    )
    matrix, diagonal = eliminate(matrix, False)
    factor = pltpu.roll(matrix * (scale * lax.rsqrt(diagonal)), 96, 1)
    factor = jnp.where(lanes < 64, factor, 0.0)
    high = factor.astype(BF16).astype(F32)
    both = jnp.where(lanes < 64, high, pltpu.roll(factor - high, 64, 1)).astype(BF16)
    factor_ref[...] = jnp.concatenate([both, both], axis=1)

    def finish(pair, carry):
        stacked = []
        for b in (2 * pair, 2 * pair + 1):
            h, l = y_high[b], y_low[b]
            stacked.append(jnp.concatenate([h, h, l, l], axis=0))
        result = jnp.dot(
            both, jnp.concatenate(stacked, axis=1), preferred_element_type=F32
        )
        out_ref[2 * pair] = result[:, :128]
        out_ref[2 * pair + 1] = result[:, 128:]
        return carry

    for copy in out_copies:
        copy.wait()
    for step in range(3):
        for half in range(2):
            if (step, half) != (0, 0):
                halo_whole(step, half).wait_send()
    for which in range(2):
        sum_whole(which, within).wait_send()
        sum_whole(which, across).wait_send()


def finish(
    factor_hbm, high_hbm, low_hbm, out_hbm, factor_ref, high, low, out,
    factor_sem, in_sem, out_sem,
):
    size = high.shape[0] // PARTS
    pieces = [pl.ds(c * size, size) for c in range(PARTS)]
    reads = [
        [
            pltpu.make_async_copy(high_hbm.at[piece], high.at[piece], in_sem.at[0, c]),
            pltpu.make_async_copy(low_hbm.at[piece], low.at[piece], in_sem.at[1, c]),
        ]
        for c, piece in enumerate(pieces)
    ]
    writes = [
        pltpu.make_async_copy(out.at[piece], out_hbm.at[piece], out_sem.at[c])
        for c, piece in enumerate(pieces)
    ]
    factor_copy = pltpu.make_async_copy(factor_hbm, factor_ref, factor_sem)
    factor_copy.start()
    for pair in reads:
        for copy in pair:
            copy.start()
    factor_copy.wait()
    factor = factor_ref[...]
    for c in range(PARTS):
        for copy in reads[c]:
            copy.wait()
        for b in range(c * size, (c + 1) * size, 2):
            stacked = [
                jnp.concatenate([high[i], high[i], low[i], low[i]], axis=0) for i in (b, b + 1)
            ]
            result = jnp.dot(
                factor, jnp.concatenate(stacked, axis=1), preferred_element_type=F32
            )
            out[b] = result[:, :128]
            out[b + 1] = result[:, 128:]
        writes[c].start()
    for copy in writes:
        copy.wait()


def shards(
    live_blocks, tile_columns, send_lists, tiles, filter_coeffs, start_block, previous_block
):
    n = lax.axis_size("rows")
    capacity, vectors, rows = start_block.shape
    fan = tile_columns.shape[1]
    _, neighbours, count = send_lists.shape
    groups = n // GROUP
    vmem = pl.BlockSpec(memory_space=pltpu.VMEM)
    hbm = pl.BlockSpec(memory_space=pl.ANY)
    half = vectors // 2
    field = pltpu.VMEM((capacity, half, rows), BF16)
    extended = pltpu.VMEM((capacity + neighbours * count, half, rows), BF16)
    wide = pltpu.VMEM((2, capacity, half, rows), F32)
    stacked = pltpu.VMEM((capacity, 2 * vectors, rows), BF16)
    scale = math.sqrt(capacity * n * rows)
    factor, high, low = pl.pallas_call(
        functools.partial(kernel, n, scale),
        out_shape=[jax.ShapeDtypeStruct((vectors, 256), BF16)]
        + [jax.ShapeDtypeStruct((capacity, 2 * vectors, rows), BF16)] * 2,
        in_specs=[hbm] * 7,
        out_specs=[vmem, hbm, hbm],
        scratch_shapes=[
            pltpu.SMEM(live_blocks.shape, jnp.int32),
            pltpu.SMEM((fan, capacity), jnp.int32),
            pltpu.SMEM((neighbours, 1, count), jnp.int32),
            pltpu.SMEM(filter_coeffs.shape, F32),
            pltpu.VMEM((capacity, vectors, rows), BF16),
            pltpu.VMEM((capacity, fan * rows, rows), BF16),
            pltpu.VMEM((capacity, vectors, rows), F32),
            *[extended] * 6,
            *[field] * 4,
            pltpu.VMEM((6 * neighbours * count, half, rows), BF16),
            wide,
            wide,
            stacked,
            stacked,
            pltpu.VMEM((vectors, 128), F32),
            pltpu.VMEM((4, 16, 128), F32),
            pltpu.VMEM((2 * (GROUP - 1), 16, 128), F32),
            pltpu.VMEM((2 * (groups - 1), 16, 128), F32),
            pltpu.SemaphoreType.DMA((5,)),
            pltpu.SemaphoreType.DMA((CHUNKS,)),
            pltpu.SemaphoreType.DMA,
            pltpu.SemaphoreType.DMA((2,)),
            pltpu.SemaphoreType.DMA((6,)),
            pltpu.SemaphoreType.DMA((6,)),
            pltpu.SemaphoreType.DMA((4,)),
            pltpu.SemaphoreType.DMA((4,)),
        ],
        compiler_params=pltpu.CompilerParams(
            collective_id=0, has_side_effects=True, vmem_limit_bytes=64 * 1024 * 1024
        ),
        name="filtered_step",
    )(
        live_blocks,
        tile_columns.T,
        jnp.transpose(send_lists, (1, 0, 2)),
        filter_coeffs,
        start_block,
        tiles.reshape(capacity, fan * rows, rows),
        previous_block,
    )
    return pl.pallas_call(
        finish,
        out_shape=jax.ShapeDtypeStruct((capacity, vectors, rows), F32),
        in_specs=[hbm, hbm, hbm],
        out_specs=hbm,
        scratch_shapes=[
            pltpu.VMEM((vectors, 256), BF16),
            stacked,
            stacked,
            pltpu.VMEM((capacity, vectors, rows), F32),
            pltpu.SemaphoreType.DMA,
            pltpu.SemaphoreType.DMA((2, PARTS)),
            pltpu.SemaphoreType.DMA((PARTS,)),
        ],
        compiler_params=pltpu.CompilerParams(vmem_limit_bytes=64 * 1024 * 1024),
        name="finish",
    )(factor, high, low)


def solution(mesh):
    return jax.shard_map(
        shards,
        mesh=mesh,
        in_specs=(
            P("rows"),
            P("rows", None),
            P("rows", None, None),
            P("rows", None, None, None),
            P(),
            P("rows", None, None),
            P("rows", None, None),
        ),
        out_specs=P("rows", None, None),
        check_vma=False,
    )
```

```python
import functools
import math

import jax
import jax.numpy as jnp
from jax import lax
from jax.experimental import pallas as pl
from jax.experimental.pallas import tpu as pltpu
from jax.sharding import PartitionSpec as P

MESH = pl.DeviceIdType.MESH
HIGHEST = lax.Precision.HIGHEST
GROUP = 8
PIVOTS = 8
PARTS = 4
BLOCKS = 24
SPAN = 12
CHUNKS = 8
F32, BF16 = jnp.float32, jnp.bfloat16


def shift_amount(which):
    return (which // 2 + 1) * (1 if which % 2 == 0 else -1)


def iota(axis):
    return lax.broadcasted_iota(jnp.int32, (32, 128), axis)


def split(value):
    high = value.astype(BF16)
    return high, (value - high.astype(F32)).astype(BF16)


def eliminate(matrix, full):
    rows = iota(0)
    diagonal = jnp.zeros((32, 128), F32)
    for start in range(0, 32, PIVOTS):
        columns = [
            jnp.broadcast_to(matrix[:, j : j + 1], (32, 128))
            for j in range(start, start + PIVOTS)
        ]
        for p in range(PIVOTS):
            j = start + p
            row, column = matrix[j : j + 1, :], columns[p]
            keep = (rows != j) if full else (rows > j)
            factor = jnp.where(keep, column * (1.0 / column[j : j + 1, :]), 0.0)
            diagonal = jnp.where(rows == j, column, diagonal)
            matrix = matrix - factor * row
            for q in range(p + 1, PIVOTS):
                columns[q] = columns[q] - factor * columns[q][j : j + 1, :]
    return matrix, diagonal


def pack(total):
    folded = total + pltpu.roll(total, 64, 1)
    return jnp.where(iota(1)[:16] < 64, folded[:16], folded[16:])


def unpack(packed):
    return jnp.concatenate([packed, pltpu.roll(packed, 64, 1)], axis=0)


def kernel(
    n, scale, live_hbm, cols_hbm, sends_hbm, coeff_hbm, start_hbm, tiles_hbm, prev_hbm,
    factor_ref, high_hbm, low_hbm,
    live_ref, cols_ref, sends_ref, coeff_ref, start_ref, tiles, prev, ext_a0, ext_b0, ext_a1, ext_b1, ext_a2, ext_b2, own_a1, own_b1, own_a2, own_b2,
    outgoing, first, accum, y_high, y_low, inverse, mine, within, across,
    entry_sem, tile_sem, prev_sem, out_sem, halo_send, halo_recv, sum_send, sum_recv,
):
    capacity = start_ref.shape[0]
    fan = cols_ref.shape[0]
    size = capacity // CHUNKS
    neighbours, _, count = sends_ref.shape
    groups = n // GROUP
    me = lax.axis_index("rows")
    ext = [[ext_a0, ext_b0], [ext_a1, ext_b1], [ext_a2, ext_b2]]
    own = [None, [own_a1, own_b1], [own_a2, own_b2]]
    def halo_target(which):
        return lax.rem(me + shift_amount(which) + n, n)

    def group_mate(k):
        return me // GROUP * GROUP + lax.rem(lax.rem(me, GROUP) + k, GROUP)

    def other_group(k):
        return lax.rem(me + k * GROUP, n)

    barrier = pltpu.get_barrier_semaphore()
    partners = [halo_target(w) for w in range(neighbours)]
    partners += [group_mate(k) for k in range(1, GROUP)]
    partners += [other_group(k) for k in range(1, groups)]
    for partner in partners:
        pl.semaphore_signal(barrier, inc=1, device_id=(partner,), device_id_type=MESH)

    def entry_copy(source, target, which):
        return pltpu.make_async_copy(source, target, entry_sem.at[which])

    entries = [
        entry_copy(*pair, i)
        for i, pair in enumerate(
            [
                (sends_hbm, sends_ref),
                (start_hbm, start_ref),
                (live_hbm, live_ref),
                (cols_hbm, cols_ref),
                (coeff_hbm, coeff_ref),
            ]
        )
    ]
    prev_copy = pltpu.make_async_copy(prev_hbm, prev, prev_sem)

    def tile_copy(c):
        piece = pl.ds(c * size, size)
        return pltpu.make_async_copy(tiles_hbm.at[piece], tiles.at[piece], tile_sem.at[c])

    for copy in entries:
        copy.start()

    def gather(step, half, which):
        base = ((step * 2 + half) * neighbours + which) * count
        for s in range(count):
            index = sends_ref[which, 0, s]
            if step == 0:
                outgoing[base + s] = start_ref[index, half * 16 : half * 16 + 16]
            else:
                outgoing[base + s] = own[step][half][index]

    def halo_copy(step, half, which):
        slot = (step * 2 + half) * neighbours + which
        return pltpu.make_async_remote_copy(
            src_ref=outgoing.at[pl.ds(slot * count, count)],
            dst_ref=ext[step][half].at[pl.ds(capacity + which * count, count)],
            send_sem=halo_send.at[step * 2 + half],
            recv_sem=halo_recv.at[step * 2 + half],
            device_id=(halo_target(which),),
            device_id_type=MESH,
        )

    def halo_whole(step, half):
        ghosts = neighbours * count
        return pltpu.make_async_remote_copy(
            src_ref=outgoing.at[pl.ds((step * 2 + half) * ghosts, ghosts)],
            dst_ref=ext[step][half].at[pl.ds(capacity, ghosts)],
            send_sem=halo_send.at[step * 2 + half],
            recv_sem=halo_recv.at[step * 2 + half],
            device_id=(halo_target(0),),
            device_id_type=MESH,
        )

    order = (4, 5, 2, 3, 0, 1)
    entries[0].wait()
    entries[1].wait()
    prev_copy.start()
    tile_copy(0).start()
    for half in range(2):
        for which in order:
            gather(0, half, which)
    pl.semaphore_wait(barrier, len(partners))
    for which in order:
        halo_copy(0, 0, which).start()

    for copy in entries[2:]:
        copy.wait()
    live = live_ref[0]

    def mask(b):
        return jnp.where(b < live, 1.0, 0.0).astype(F32)

    def fill(b, carry):
        value = (start_ref[b].astype(F32) * mask(b)).astype(BF16)
        ext_a0[b] = value[:16]
        ext_b0[b] = value[16:]
        return carry

    lax.fori_loop(0, capacity, fill, 0, unroll=4)

    def within_copy(which, k):
        return pltpu.make_async_remote_copy(
            src_ref=mine.at[2 * which],
            dst_ref=within.at[which * (GROUP - 1) + k - 1],
            send_sem=sum_send.at[2 * which],
            recv_sem=sum_recv.at[2 * which],
            device_id=(group_mate(k),),
            device_id_type=MESH,
        )

    def across_copy(which, k):
        return pltpu.make_async_remote_copy(
            src_ref=mine.at[2 * which + 1],
            dst_ref=across.at[which * (groups - 1) + k - 1],
            send_sem=sum_send.at[2 * which + 1],
            recv_sem=sum_recv.at[2 * which + 1],
            device_id=(other_group(k),),
            device_id_type=MESH,
        )

    def sum_whole(which, landing):
        peers = landing.shape[0] // 2
        slot = 2 * which + (0 if landing is within else 1)
        return pltpu.make_async_remote_copy(
            src_ref=landing.at[pl.ds(which * peers, peers)],
            dst_ref=landing.at[pl.ds(which * peers, peers)],
            send_sem=sum_send.at[slot],
            recv_sem=sum_recv.at[slot],
            device_id=(group_mate(1),),
            device_id_type=MESH,
        )

    def sum_start(which, value):
        mine[2 * which] = value
        for k in range(1, GROUP):
            within_copy(which, k).start()

    def sum_middle(which):
        total = mine[2 * which]
        sum_whole(which, within).wait_recv()
        for k in range(1, GROUP):
            total += within[which * (GROUP - 1) + k - 1]
        mine[2 * which + 1] = total
        for k in range(1, groups):
            across_copy(which, k).start()

    def sum_end(which):
        total = mine[2 * which + 1]
        sum_whole(which, across).wait_recv()
        for k in range(1, groups):
            total += across[which * (groups - 1) + k - 1]
        return total

    rows_dot = functools.partial(
        lax.dot_general, dimension_numbers=(((1,), (1,)), ((), ())), preferred_element_type=F32
    )

    prev_copy.wait()
    for c in range(1, CHUNKS):
        tile_copy(c).start()

    def prev_gram(pair, total):
        left, right = [], []
        for b in (2 * pair, 2 * pair + 1):
            high, low = split(prev[b] * mask(b))
            y_high[b, :32] = high
            y_low[b, :32] = low
            left.append(jnp.concatenate([high, low], axis=0))
            right.append(jnp.concatenate([high, high, low, low], axis=0))
        return total + rows_dot(
            jnp.concatenate(left, axis=1), jnp.concatenate(right, axis=1)
        )

    total = lax.fori_loop(0, capacity // 2, prev_gram, jnp.zeros((64, 128), F32), unroll=2)
    sum_start(0, pack(total[:32] + total[32:]))
    halo_whole(0, 0).wait_send()
    for which in order:
        halo_copy(0, 1, which).start()

    def product(step, half, b):
        vectors = ext[step][half]
        picked = jnp.concatenate([vectors[cols_ref[k, b]] for k in range(fan)], axis=1)
        return jnp.dot(picked, tiles[b], preferred_element_type=F32) * mask(b)

    c0, c1, c2, c3 = (coeff_ref[i] for i in range(4))

    def first_step(half, b):
        result = product(0, half, b)
        rounded = result.astype(BF16)
        first[half, b] = result
        own[1][half][b] = rounded
        ext[1][half][b] = rounded

    def second_step(half, b):
        before = ext[0][half][b].astype(F32)
        one = first[half, b]
        result = 2.0 * product(1, half, b) - before
        rounded = result.astype(BF16)
        own[2][half][b] = rounded
        ext[2][half][b] = rounded
        accum[half, b] = c0 * before + (c1 - c3) * one + c2 * result

    def third_step(half, b):
        rows = slice(32 + 16 * half, 48 + 16 * half)
        high, low = split(accum[half, b] + (2.0 * c3) * product(2, half, b))
        y_high[b, rows] = high
        y_low[b, rows] = low

    def await_halo(step, half):
        halo_whole(step, half).wait_recv()

    def loop(body, lower, upper):
        def one(b, carry):
            body(b)
            return carry

        lax.fori_loop(lower, upper, one, 0, unroll=BLOCKS)

    for half in range(2):
        await_halo(0, half)
        if half == 0:
            for c in range(CHUNKS):
                tile_copy(c).wait()
        loop(functools.partial(first_step, half), 0, capacity)
        for which in order:
            gather(1, half, which)
            halo_copy(1, half, which).start()
        if half == 0:
            sum_middle(0)

    rows, lanes = iota(0), iota(1)
    gram = unpack(sum_end(0))
    matrix = jnp.where(lanes < 32, gram, jnp.where(lanes == rows + 64, 1.0, 0.0))
    matrix, diagonal = eliminate(matrix, True)
    middle = (lanes >= 32) & (lanes < 64)
    inverse[...] = jnp.where(middle, pltpu.roll(matrix / diagonal, 96, 1), 0.0)

    for half in range(2):
        await_halo(1, half)
        loop(functools.partial(second_step, half), 0, capacity)
        for which in order:
            gather(2, half, which)
            halo_copy(2, half, which).start()

    await_halo(2, 0)
    def third_group(half, group):
        for i in range(SPAN):
            third_step(half, group * SPAN + i)

    def filtered_gram(group, total):
        for i in range(0, SPAN, 2):
            left, right = [], []
            for b in (group * SPAN + i, group * SPAN + i + 1):
                left.append(jnp.concatenate([y_high[b, 32:64], y_low[b, 32:64]], axis=0))
                right.append(jnp.concatenate([y_high[b], y_low[b]], axis=0))
            total += rows_dot(
                jnp.concatenate(left, axis=1), jnp.concatenate(right, axis=1)
            )
        return total

    def last_group(group, total):
        total = filtered_gram(group - 1, total)
        third_group(1, group)
        return total

    loop(functools.partial(third_step, 0), 0, capacity)
    await_halo(2, 1)
    third_group(1, 0)
    total = lax.fori_loop(1, capacity // SPAN, last_group, jnp.zeros((64, 128), F32))
    total = filtered_gram(capacity // SPAN - 1, total)
    out_copies = [
        pltpu.make_async_copy(y_high, high_hbm, out_sem.at[0]),
        pltpu.make_async_copy(y_low, low_hbm, out_sem.at[1]),
    ]
    sum_start(1, pack(total[:32] + total[32:]))
    for copy in out_copies:
        copy.start()
    sum_middle(1)
    sums = unpack(sum_end(1))

    cross = jnp.where(lanes < 32, sums, 0.0)
    below = jnp.zeros((96, 128), F32)
    coeff = jnp.dot(
        cross, jnp.concatenate([inverse[...], below], axis=0),
        precision=HIGHEST, preferred_element_type=F32,
    )
    removed = rows_dot(
        coeff, jnp.concatenate([pltpu.roll(cross, 32, 1), below], axis=0), precision=HIGHEST
    )
    matrix = jnp.where(
        lanes < 32,
        pltpu.roll(sums, 96, 1) - removed,
        jnp.where(lanes < 64, -coeff, jnp.where(lanes == rows + 64, 1.0, 0.0)),
    )
    matrix, diagonal = eliminate(matrix, False)
    factor = pltpu.roll(matrix * (scale * lax.rsqrt(diagonal)), 96, 1)
    factor = jnp.where(lanes < 64, factor, 0.0)
    high = factor.astype(BF16).astype(F32)
    both = jnp.where(lanes < 64, high, pltpu.roll(factor - high, 64, 1)).astype(BF16)
    factor_ref[...] = jnp.concatenate([both, both], axis=1)

    def finish(pair, carry):
        stacked = []
        for b in (2 * pair, 2 * pair + 1):
            h, l = y_high[b], y_low[b]
            stacked.append(jnp.concatenate([h, h, l, l], axis=0))
        result = jnp.dot(
            both, jnp.concatenate(stacked, axis=1), preferred_element_type=F32
        )
        out_ref[2 * pair] = result[:, :128]
        out_ref[2 * pair + 1] = result[:, 128:]
        return carry

    for copy in out_copies:
        copy.wait()
    for step in range(3):
        for half in range(2):
            if (step, half) != (0, 0):
                halo_whole(step, half).wait_send()
    for which in range(2):
        sum_whole(which, within).wait_send()
        sum_whole(which, across).wait_send()


def finish(
    factor_hbm, high_hbm, low_hbm, out_hbm, factor_ref, high, low, out,
    factor_sem, in_sem, out_sem,
):
    size = high.shape[0] // PARTS
    pieces = [pl.ds(c * size, size) for c in range(PARTS)]
    reads = [
        [
            pltpu.make_async_copy(high_hbm.at[piece], high.at[piece], in_sem.at[0, c]),
            pltpu.make_async_copy(low_hbm.at[piece], low.at[piece], in_sem.at[1, c]),
        ]
        for c, piece in enumerate(pieces)
    ]
    writes = [
        pltpu.make_async_copy(out.at[piece], out_hbm.at[piece], out_sem.at[c])
        for c, piece in enumerate(pieces)
    ]
    factor_copy = pltpu.make_async_copy(factor_hbm, factor_ref, factor_sem)
    factor_copy.start()
    for pair in reads:
        for copy in pair:
            copy.start()
    factor_copy.wait()
    factor = factor_ref[...]
    for c in range(PARTS):
        for copy in reads[c]:
            copy.wait()
        for b in range(c * size, (c + 1) * size, 2):
            stacked = [
                jnp.concatenate([high[i], high[i], low[i], low[i]], axis=0) for i in (b, b + 1)
            ]
            result = jnp.dot(
                factor, jnp.concatenate(stacked, axis=1), preferred_element_type=F32
            )
            out[b] = result[:, :128]
            out[b + 1] = result[:, 128:]
        writes[c].start()
    for copy in writes:
        copy.wait()


def shards(
    live_blocks, tile_columns, send_lists, tiles, filter_coeffs, start_block, previous_block
):
    n = lax.axis_size("rows")
    capacity, vectors, rows = start_block.shape
    fan = tile_columns.shape[1]
    _, neighbours, count = send_lists.shape
    groups = n // GROUP
    vmem = pl.BlockSpec(memory_space=pltpu.VMEM)
    hbm = pl.BlockSpec(memory_space=pl.ANY)
    half = vectors // 2
    field = pltpu.VMEM((capacity, half, rows), BF16)
    extended = pltpu.VMEM((capacity + neighbours * count, half, rows), BF16)
    wide = pltpu.VMEM((2, capacity, half, rows), F32)
    stacked = pltpu.VMEM((capacity, 2 * vectors, rows), BF16)
    scale = math.sqrt(capacity * n * rows)
    factor, high, low = pl.pallas_call(
        functools.partial(kernel, n, scale),
        out_shape=[jax.ShapeDtypeStruct((vectors, 256), BF16)]
        + [jax.ShapeDtypeStruct((capacity, 2 * vectors, rows), BF16)] * 2,
        in_specs=[hbm] * 7,
        out_specs=[vmem, hbm, hbm],
        scratch_shapes=[
            pltpu.SMEM(live_blocks.shape, jnp.int32),
            pltpu.SMEM((fan, capacity), jnp.int32),
            pltpu.SMEM((neighbours, 1, count), jnp.int32),
            pltpu.SMEM(filter_coeffs.shape, F32),
            pltpu.VMEM((capacity, vectors, rows), BF16),
            pltpu.VMEM((capacity, fan * rows, rows), BF16),
            pltpu.VMEM((capacity, vectors, rows), F32),
            *[extended] * 6,
            *[field] * 4,
            pltpu.VMEM((6 * neighbours * count, half, rows), BF16),
            wide,
            wide,
            stacked,
            stacked,
            pltpu.VMEM((vectors, 128), F32),
            pltpu.VMEM((4, 16, 128), F32),
            pltpu.VMEM((2 * (GROUP - 1), 16, 128), F32),
            pltpu.VMEM((2 * (groups - 1), 16, 128), F32),
            pltpu.SemaphoreType.DMA((5,)),
            pltpu.SemaphoreType.DMA((CHUNKS,)),
            pltpu.SemaphoreType.DMA,
            pltpu.SemaphoreType.DMA((2,)),
            pltpu.SemaphoreType.DMA((6,)),
            pltpu.SemaphoreType.DMA((6,)),
            pltpu.SemaphoreType.DMA((4,)),
            pltpu.SemaphoreType.DMA((4,)),
        ],
        compiler_params=pltpu.CompilerParams(
            collective_id=0, has_side_effects=True, vmem_limit_bytes=64 * 1024 * 1024
        ),
        name="filtered_step",
    )(
        live_blocks,
        tile_columns.T,
        jnp.transpose(send_lists, (1, 0, 2)),
        filter_coeffs,
        start_block,
        tiles.reshape(capacity, fan * rows, rows),
        previous_block,
    )
    return pl.pallas_call(
        finish,
        out_shape=jax.ShapeDtypeStruct((capacity, vectors, rows), F32),
        in_specs=[hbm, hbm, hbm],
        out_specs=hbm,
        scratch_shapes=[
            pltpu.VMEM((vectors, 256), BF16),
            stacked,
            stacked,
            pltpu.VMEM((capacity, vectors, rows), F32),
            pltpu.SemaphoreType.DMA,
            pltpu.SemaphoreType.DMA((2, PARTS)),
            pltpu.SemaphoreType.DMA((PARTS,)),
        ],
        compiler_params=pltpu.CompilerParams(vmem_limit_bytes=64 * 1024 * 1024),
        name="finish",
    )(factor, high, low)


def solution(mesh):
    return jax.shard_map(
        shards,
        mesh=mesh,
        in_specs=(
            P("rows"),
            P("rows", None),
            P("rows", None, None),
            P("rows", None, None, None),
            P(),
            P("rows", None, None),
            P("rows", None, None),
        ),
        out_specs=P("rows", None, None),
        check_vma=False,
    )
```

```python
import functools
import math

import jax
import jax.numpy as jnp
from jax import lax
from jax.experimental import pallas as pl
from jax.experimental.pallas import tpu as pltpu
from jax.sharding import PartitionSpec as P

MESH = pl.DeviceIdType.MESH
HIGHEST = lax.Precision.HIGHEST
GROUP = 8
PIVOTS = 8
PARTS = 3
BLOCKS = 24
SPAN = 24
CHUNKS = 8
F32, BF16 = jnp.float32, jnp.bfloat16

rows_dot = functools.partial(
    lax.dot_general, dimension_numbers=(((1,), (1,)), ((), ())), preferred_element_type=F32
)


def shift_amount(which):
    return (which // 2 + 1) * (1 if which % 2 == 0 else -1)


def iota(axis):
    return lax.broadcasted_iota(jnp.int32, (32, 128), axis)


def split(value):
    high = value.astype(BF16)
    return high, (value - high.astype(F32)).astype(BF16)


def eliminate(matrix, full):
    rows = iota(0)
    diagonal = jnp.zeros((32, 128), F32)
    for start in range(0, 32, PIVOTS):
        columns = [
            jnp.broadcast_to(matrix[:, j : j + 1], (32, 128))
            for j in range(start, start + PIVOTS)
        ]
        for p in range(PIVOTS):
            j = start + p
            row, column = matrix[j : j + 1, :], columns[p]
            keep = (rows != j) if full else (rows > j)
            factor = jnp.where(keep, column * (1.0 / column[j : j + 1, :]), 0.0)
            diagonal = jnp.where(rows == j, column, diagonal)
            matrix = matrix - factor * row
            for q in range(p + 1, PIVOTS):
                columns[q] = columns[q] - factor * columns[q][j : j + 1, :]
    return matrix, diagonal


def pack(total):
    folded = total + pltpu.roll(total, 64, 1)
    return jnp.where(iota(1)[:16] < 64, folded[:16], folded[16:])


def unpack(packed):
    return jnp.concatenate([packed, pltpu.roll(packed, 64, 1)], axis=0)


def solve(scale, state):
    rows, lanes = iota(0), iota(1)
    sums = state[32:]
    cross = jnp.where(lanes < 32, sums, 0.0)
    below = jnp.zeros((96, 128), F32)
    coeff = jnp.dot(
        cross, jnp.concatenate([state[:32], below], axis=0),
        precision=HIGHEST, preferred_element_type=F32,
    )
    removed = rows_dot(
        coeff, jnp.concatenate([pltpu.roll(cross, 32, 1), below], axis=0), precision=HIGHEST
    )
    matrix = jnp.where(
        lanes < 32,
        pltpu.roll(sums, 96, 1) - removed,
        jnp.where(lanes < 64, -coeff, jnp.where(lanes == rows + 64, 1.0, 0.0)),
    )
    matrix, diagonal = eliminate(matrix, False)
    factor = pltpu.roll(matrix * (scale * lax.rsqrt(diagonal)), 96, 1)
    factor = jnp.where(lanes < 64, factor, 0.0)
    high = factor.astype(BF16).astype(F32)
    both = jnp.where(lanes < 64, high, pltpu.roll(factor - high, 64, 1)).astype(BF16)
    return jnp.concatenate([both, both], axis=1)


def kernel(
    n, live_hbm, cols_hbm, sends_hbm, coeff_hbm, start_hbm, tiles_hbm, prev_hbm,
    state_ref, high_hbm, low_hbm,
    live_ref, cols_ref, sends_ref, coeff_ref, start_ref, tiles, prev, ext_a0, ext_b0, ext_a1, ext_b1, ext_a2, ext_b2, own_a1, own_b1, own_a2, own_b2,
    outgoing, first, accum, y_high, y_low, mine, within, across,
    entry_sem, tile_sem, prev_sem, out_sem, halo_send, halo_recv, sum_send, sum_recv,
):
    capacity = start_ref.shape[0]
    fan = cols_ref.shape[0]
    size = capacity // CHUNKS
    neighbours, _, count = sends_ref.shape
    groups = n // GROUP
    me = lax.axis_index("rows")
    ext = [[ext_a0, ext_b0], [ext_a1, ext_b1], [ext_a2, ext_b2]]
    own = [None, [own_a1, own_b1], [own_a2, own_b2]]
    def halo_target(which):
        return lax.rem(me + shift_amount(which) + n, n)

    def group_mate(k):
        return me // GROUP * GROUP + lax.rem(lax.rem(me, GROUP) + k, GROUP)

    def other_group(k):
        return lax.rem(me + k * GROUP, n)

    barrier = pltpu.get_barrier_semaphore()
    partners = [halo_target(w) for w in range(neighbours)]
    partners += [group_mate(k) for k in range(1, GROUP)]
    partners += [other_group(k) for k in range(1, groups)]
    for partner in partners:
        pl.semaphore_signal(barrier, inc=1, device_id=(partner,), device_id_type=MESH)

    def entry_copy(source, target, which):
        return pltpu.make_async_copy(source, target, entry_sem.at[which])

    entries = [
        entry_copy(*pair, i)
        for i, pair in enumerate(
            [
                (sends_hbm, sends_ref),
                (start_hbm, start_ref),
                (live_hbm, live_ref),
                (cols_hbm, cols_ref),
                (coeff_hbm, coeff_ref),
            ]
        )
    ]
    prev_copy = pltpu.make_async_copy(prev_hbm, prev, prev_sem)

    def tile_copy(c):
        piece = pl.ds(c * size, size)
        return pltpu.make_async_copy(tiles_hbm.at[piece], tiles.at[piece], tile_sem.at[c])

    for copy in entries:
        copy.start()

    def gather(step, half, which):
        base = ((step * 2 + half) * neighbours + which) * count
        for s in range(count):
            index = sends_ref[which, 0, s]
            if step == 0:
                outgoing[base + s] = start_ref[index, half * 16 : half * 16 + 16]
            else:
                outgoing[base + s] = own[step][half][index]

    def halo_copy(step, half, which):
        slot = (step * 2 + half) * neighbours + which
        return pltpu.make_async_remote_copy(
            src_ref=outgoing.at[pl.ds(slot * count, count)],
            dst_ref=ext[step][half].at[pl.ds(capacity + which * count, count)],
            send_sem=halo_send.at[step * 2 + half],
            recv_sem=halo_recv.at[step * 2 + half],
            device_id=(halo_target(which),),
            device_id_type=MESH,
        )

    def halo_whole(step, half):
        ghosts = neighbours * count
        return pltpu.make_async_remote_copy(
            src_ref=outgoing.at[pl.ds((step * 2 + half) * ghosts, ghosts)],
            dst_ref=ext[step][half].at[pl.ds(capacity, ghosts)],
            send_sem=halo_send.at[step * 2 + half],
            recv_sem=halo_recv.at[step * 2 + half],
            device_id=(halo_target(0),),
            device_id_type=MESH,
        )

    order = (4, 5, 2, 3, 0, 1)
    entries[0].wait()
    entries[1].wait()
    prev_copy.start()
    tile_copy(0).start()
    for half in range(2):
        for which in order:
            gather(0, half, which)
    pl.semaphore_wait(barrier, len(partners))
    for which in order:
        halo_copy(0, 0, which).start()

    for copy in entries[2:]:
        copy.wait()
    live = live_ref[0]

    def mask(b):
        return jnp.where(b < live, 1.0, 0.0).astype(F32)

    def fill(b, carry):
        value = (start_ref[b].astype(F32) * mask(b)).astype(BF16)
        ext_a0[b] = value[:16]
        ext_b0[b] = value[16:]
        return carry

    lax.fori_loop(0, capacity, fill, 0, unroll=4)

    def within_copy(which, k):
        return pltpu.make_async_remote_copy(
            src_ref=mine.at[2 * which],
            dst_ref=within.at[which * (GROUP - 1) + k - 1],
            send_sem=sum_send.at[2 * which],
            recv_sem=sum_recv.at[2 * which],
            device_id=(group_mate(k),),
            device_id_type=MESH,
        )

    def across_copy(which, k):
        return pltpu.make_async_remote_copy(
            src_ref=mine.at[2 * which + 1],
            dst_ref=across.at[which * (groups - 1) + k - 1],
            send_sem=sum_send.at[2 * which + 1],
            recv_sem=sum_recv.at[2 * which + 1],
            device_id=(other_group(k),),
            device_id_type=MESH,
        )

    def sum_whole(which, landing):
        peers = landing.shape[0] // 2
        slot = 2 * which + (0 if landing is within else 1)
        return pltpu.make_async_remote_copy(
            src_ref=landing.at[pl.ds(which * peers, peers)],
            dst_ref=landing.at[pl.ds(which * peers, peers)],
            send_sem=sum_send.at[slot],
            recv_sem=sum_recv.at[slot],
            device_id=(group_mate(1),),
            device_id_type=MESH,
        )

    def sum_start(which, value):
        mine[2 * which] = value
        for k in range(1, GROUP):
            within_copy(which, k).start()

    def sum_middle(which):
        total = mine[2 * which]
        sum_whole(which, within).wait_recv()
        for k in range(1, GROUP):
            total += within[which * (GROUP - 1) + k - 1]
        mine[2 * which + 1] = total
        for k in range(1, groups):
            across_copy(which, k).start()

    def sum_end(which):
        total = mine[2 * which + 1]
        sum_whole(which, across).wait_recv()
        for k in range(1, groups):
            total += across[which * (groups - 1) + k - 1]
        return total

    prev_copy.wait()
    for c in range(1, CHUNKS):
        tile_copy(c).start()

    def prev_gram(pair, total):
        left, right = [], []
        for b in (2 * pair, 2 * pair + 1):
            high, low = split(prev[b] * mask(b))
            y_high[b, :32] = high
            y_low[b, :32] = low
            left.append(jnp.concatenate([high, low], axis=0))
            right.append(jnp.concatenate([high, high, low, low], axis=0))
        return total + rows_dot(
            jnp.concatenate(left, axis=1), jnp.concatenate(right, axis=1)
        )

    total = lax.fori_loop(0, capacity // 2, prev_gram, jnp.zeros((64, 128), F32), unroll=2)
    sum_start(0, pack(total[:32] + total[32:]))
    halo_whole(0, 0).wait_send()
    for which in order:
        halo_copy(0, 1, which).start()

    def product(step, half, b):
        vectors = ext[step][half]
        picked = jnp.concatenate([vectors[cols_ref[k, b]] for k in range(fan)], axis=1)
        return jnp.dot(picked, tiles[b], preferred_element_type=F32) * mask(b)

    c0, c1, c2, c3 = (coeff_ref[i] for i in range(4))

    def first_step(half, b):
        result = product(0, half, b)
        rounded = result.astype(BF16)
        first[half, b] = result
        own[1][half][b] = rounded
        ext[1][half][b] = rounded

    def second_step(half, b):
        before = ext[0][half][b].astype(F32)
        one = first[half, b]
        result = 2.0 * product(1, half, b) - before
        rounded = result.astype(BF16)
        own[2][half][b] = rounded
        ext[2][half][b] = rounded
        accum[half, b] = c0 * before + (c1 - c3) * one + c2 * result

    def third_step(half, b):
        rows = slice(32 + 16 * half, 48 + 16 * half)
        high, low = split(accum[half, b] + (2.0 * c3) * product(2, half, b))
        y_high[b, rows] = high
        y_low[b, rows] = low

    def await_halo(step, half):
        halo_whole(step, half).wait_recv()

    def loop(body, lower, upper):
        def one(b, carry):
            body(b)
            return carry

        lax.fori_loop(lower, upper, one, 0, unroll=BLOCKS)

    for half in range(2):
        await_halo(0, half)
        if half == 0:
            for c in range(CHUNKS):
                tile_copy(c).wait()
        loop(functools.partial(first_step, half), 0, capacity)
        for which in order:
            gather(1, half, which)
        if half == 0:
            halo_whole(0, 1).wait_send()
        for which in order:
            halo_copy(1, half, which).start()
        if half == 0:
            sum_middle(0)

    rows, lanes = iota(0), iota(1)
    gram = unpack(sum_end(0))
    matrix = jnp.where(lanes < 32, gram, jnp.where(lanes == rows + 64, 1.0, 0.0))
    matrix, diagonal = eliminate(matrix, True)
    middle = (lanes >= 32) & (lanes < 64)
    state_ref[:32] = jnp.where(middle, pltpu.roll(matrix / diagonal, 96, 1), 0.0)

    for half in range(2):
        await_halo(1, half)
        loop(functools.partial(second_step, half), 0, capacity)
        for which in order:
            gather(2, half, which)
            halo_copy(2, half, which).start()

    await_halo(2, 0)
    def third_group(half, group):
        for i in range(SPAN):
            third_step(half, group * SPAN + i)

    def filtered_gram(group, total):
        for i in range(0, SPAN, 2):
            left, right = [], []
            for b in (group * SPAN + i, group * SPAN + i + 1):
                left.append(jnp.concatenate([y_high[b, 32:64], y_low[b, 32:64]], axis=0))
                right.append(jnp.concatenate([y_high[b], y_low[b]], axis=0))
            total += rows_dot(
                jnp.concatenate(left, axis=1), jnp.concatenate(right, axis=1)
            )
        return total

    def last_group(group, total):
        total = filtered_gram(group - 1, total)
        third_group(1, group)
        return total

    loop(functools.partial(third_step, 0), 0, capacity)
    await_halo(2, 1)
    third_group(1, 0)
    total = lax.fori_loop(1, capacity // SPAN, last_group, jnp.zeros((64, 128), F32))
    total = filtered_gram(capacity // SPAN - 1, total)
    out_copies = [
        pltpu.make_async_copy(y_high, high_hbm, out_sem.at[0]),
        pltpu.make_async_copy(y_low, low_hbm, out_sem.at[1]),
    ]
    sum_start(1, pack(total[:32] + total[32:]))
    for copy in out_copies:
        copy.start()
    sum_middle(1)
    state_ref[32:] = unpack(sum_end(1))
    for copy in out_copies:
        copy.wait()
    for step in range(1, 3):
        for half in range(2):
            halo_whole(step, half).wait_send()
    for which in range(2):
        sum_whole(which, within).wait_send()
        sum_whole(which, across).wait_send()


def finish(
    scale, state_hbm, high_hbm, low_hbm, out_hbm, state, high, low, out,
    state_sem, in_sem, out_sem,
):
    size = high.shape[0] // PARTS
    pieces = [pl.ds(c * size, size) for c in range(PARTS)]
    reads = [
        [
            pltpu.make_async_copy(high_hbm.at[piece], high.at[piece], in_sem.at[0, c]),
            pltpu.make_async_copy(low_hbm.at[piece], low.at[piece], in_sem.at[1, c]),
        ]
        for c, piece in enumerate(pieces)
    ]
    writes = [
        pltpu.make_async_copy(out.at[piece], out_hbm.at[piece], out_sem.at[c])
        for c, piece in enumerate(pieces)
    ]
    state_copy = pltpu.make_async_copy(state_hbm, state, state_sem)
    state_copy.start()
    state_copy.wait()
    for pair in reads:
        for copy in pair:
            copy.start()
    factor = solve(scale, state[...])
    for c in range(PARTS):
        for copy in reads[c]:
            copy.wait()
        for b in range(c * size, (c + 1) * size, 2):
            stacked = [
                jnp.concatenate([high[i], high[i], low[i], low[i]], axis=0) for i in (b, b + 1)
            ]
            result = jnp.dot(
                factor, jnp.concatenate(stacked, axis=1), preferred_element_type=F32
            )
            out[b] = result[:, :128]
            out[b + 1] = result[:, 128:]
        writes[c].start()
    for copy in writes:
        copy.wait()


def shards(
    live_blocks, tile_columns, send_lists, tiles, filter_coeffs, start_block, previous_block
):
    n = lax.axis_size("rows")
    capacity, vectors, rows = start_block.shape
    fan = tile_columns.shape[1]
    _, neighbours, count = send_lists.shape
    groups = n // GROUP
    vmem = pl.BlockSpec(memory_space=pltpu.VMEM)
    hbm = pl.BlockSpec(memory_space=pl.ANY)
    half = vectors // 2
    field = pltpu.VMEM((capacity, half, rows), BF16)
    extended = pltpu.VMEM((capacity + neighbours * count, half, rows), BF16)
    wide = pltpu.VMEM((2, capacity, half, rows), F32)
    stacked = pltpu.VMEM((capacity, 2 * vectors, rows), BF16)
    scale = math.sqrt(capacity * n * rows)
    state, high, low = pl.pallas_call(
        functools.partial(kernel, n),
        out_shape=[jax.ShapeDtypeStruct((2 * vectors, 128), F32)]
        + [jax.ShapeDtypeStruct((capacity, 2 * vectors, rows), BF16)] * 2,
        in_specs=[hbm] * 7,
        out_specs=[vmem, hbm, hbm],
        scratch_shapes=[
            pltpu.SMEM(live_blocks.shape, jnp.int32),
            pltpu.SMEM((fan, capacity), jnp.int32),
            pltpu.SMEM((neighbours, 1, count), jnp.int32),
            pltpu.SMEM(filter_coeffs.shape, F32),
            pltpu.VMEM((capacity, vectors, rows), BF16),
            pltpu.VMEM((capacity, fan * rows, rows), BF16),
            pltpu.VMEM((capacity, vectors, rows), F32),
            *[extended] * 6,
            *[field] * 4,
            pltpu.VMEM((6 * neighbours * count, half, rows), BF16),
            wide,
            wide,
            stacked,
            stacked,
            pltpu.VMEM((4, 16, 128), F32),
            pltpu.VMEM((2 * (GROUP - 1), 16, 128), F32),
            pltpu.VMEM((2 * (groups - 1), 16, 128), F32),
            pltpu.SemaphoreType.DMA((5,)),
            pltpu.SemaphoreType.DMA((CHUNKS,)),
            pltpu.SemaphoreType.DMA,
            pltpu.SemaphoreType.DMA((2,)),
            pltpu.SemaphoreType.DMA((6,)),
            pltpu.SemaphoreType.DMA((6,)),
            pltpu.SemaphoreType.DMA((4,)),
            pltpu.SemaphoreType.DMA((4,)),
        ],
        compiler_params=pltpu.CompilerParams(
            collective_id=0, has_side_effects=True, vmem_limit_bytes=64 * 1024 * 1024
        ),
        name="filtered_step",
    )(
        live_blocks,
        tile_columns.T,
        jnp.transpose(send_lists, (1, 0, 2)),
        filter_coeffs,
        start_block,
        tiles.reshape(capacity, fan * rows, rows),
        previous_block,
    )
    return pl.pallas_call(
        functools.partial(finish, scale),
        out_shape=jax.ShapeDtypeStruct((capacity, vectors, rows), F32),
        in_specs=[hbm, hbm, hbm],
        out_specs=hbm,
        scratch_shapes=[
            pltpu.VMEM((2 * vectors, 128), F32),
            stacked,
            stacked,
            pltpu.VMEM((capacity, vectors, rows), F32),
            pltpu.SemaphoreType.DMA,
            pltpu.SemaphoreType.DMA((2, PARTS)),
            pltpu.SemaphoreType.DMA((PARTS,)),
        ],
        compiler_params=pltpu.CompilerParams(vmem_limit_bytes=64 * 1024 * 1024),
        name="finish",
    )(state, high, low)


def solution(mesh):
    return jax.shard_map(
        shards,
        mesh=mesh,
        in_specs=(
            P("rows"),
            P("rows", None),
            P("rows", None, None),
            P("rows", None, None, None),
            P(),
            P("rows", None, None),
            P("rows", None, None),
        ),
        out_specs=P("rows", None, None),
        check_vma=False,
    )
```

```python
import functools
import math

import jax
import jax.numpy as jnp
from jax import lax
from jax.experimental import pallas as pl
from jax.experimental.pallas import tpu as pltpu
from jax.sharding import PartitionSpec as P

MESH = pl.DeviceIdType.MESH
HIGHEST = lax.Precision.HIGHEST
GROUP = 8
PIVOTS = 8
PARTS = 3
BLOCKS = 24
SPAN = 24
CHUNKS = 8
F32, BF16 = jnp.float32, jnp.bfloat16

rows_dot = functools.partial(
    lax.dot_general, dimension_numbers=(((1,), (1,)), ((), ())), preferred_element_type=F32
)


def shift_amount(which):
    return (which // 2 + 1) * (1 if which % 2 == 0 else -1)


def iota(axis):
    return lax.broadcasted_iota(jnp.int32, (32, 128), axis)


def split(value):
    high = value.astype(BF16)
    return high, (value - high.astype(F32)).astype(BF16)


def eliminate(matrix, full):
    rows = iota(0)
    diagonal = jnp.zeros((32, 128), F32)
    for start in range(0, 32, PIVOTS):
        columns = [
            jnp.broadcast_to(matrix[:, j : j + 1], (32, 128))
            for j in range(start, start + PIVOTS)
        ]
        for p in range(PIVOTS):
            j = start + p
            row, column = matrix[j : j + 1, :], columns[p]
            keep = (rows != j) if full else (rows > j)
            factor = jnp.where(keep, column * (1.0 / column[j : j + 1, :]), 0.0)
            diagonal = jnp.where(rows == j, column, diagonal)
            matrix = matrix - factor * row
            for q in range(p + 1, PIVOTS):
                columns[q] = columns[q] - factor * columns[q][j : j + 1, :]
    return matrix, diagonal


def pack(total):
    folded = total + pltpu.roll(total, 64, 1)
    return jnp.where(iota(1)[:16] < 64, folded[:16], folded[16:])


def unpack(packed):
    return jnp.concatenate([packed, pltpu.roll(packed, 64, 1)], axis=0)


def solve(scale, state):
    rows, lanes = iota(0), iota(1)
    sums = state[32:]
    cross = jnp.where(lanes < 32, sums, 0.0)
    below = jnp.zeros((96, 128), F32)
    coeff = jnp.dot(
        cross, jnp.concatenate([state[:32], below], axis=0),
        precision=HIGHEST, preferred_element_type=F32,
    )
    removed = rows_dot(
        coeff, jnp.concatenate([pltpu.roll(cross, 32, 1), below], axis=0), precision=HIGHEST
    )
    matrix = jnp.where(
        lanes < 32,
        pltpu.roll(sums, 96, 1) - removed,
        jnp.where(lanes < 64, -coeff, jnp.where(lanes == rows + 64, 1.0, 0.0)),
    )
    matrix, diagonal = eliminate(matrix, False)
    factor = pltpu.roll(matrix * (scale * lax.rsqrt(diagonal)), 96, 1)
    factor = jnp.where(lanes < 64, factor, 0.0)
    high = factor.astype(BF16).astype(F32)
    both = jnp.where(lanes < 64, high, pltpu.roll(factor - high, 64, 1)).astype(BF16)
    return jnp.concatenate([both, both], axis=1)


def kernel(
    n, live_hbm, cols_hbm, sends_hbm, coeff_hbm, start_hbm, tiles_hbm, prev_hbm,
    state_ref, high_hbm, low_hbm,
    live_ref, cols_ref, sends_ref, coeff_ref, start_a, start_b, tiles, prev, ext_a0, ext_b0, ext_a1, ext_b1, ext_a2, ext_b2, own_a1, own_b1, own_a2, own_b2,
    outgoing, first, accum, y_high, y_low, mine, within, across,
    entry_sem, tile_sem, prev_sem, out_sem, halo_send, halo_recv, sum_send, sum_recv,
):
    capacity = start_a.shape[0]
    fan = cols_ref.shape[0]
    size = capacity // CHUNKS
    neighbours, _, count = sends_ref.shape
    groups = n // GROUP
    me = lax.axis_index("rows")
    ext = [[ext_a0, ext_b0], [ext_a1, ext_b1], [ext_a2, ext_b2]]
    own = [None, [own_a1, own_b1], [own_a2, own_b2]]
    def entry_copy(source, target, which):
        return pltpu.make_async_copy(source, target, entry_sem.at[which])

    entries = [
        entry_copy(*pair, i)
        for i, pair in enumerate(
            [
                (sends_hbm, sends_ref),
                (start_hbm.at[:, :16], start_a),
                (start_hbm.at[:, 16:], start_b),
                (live_hbm, live_ref),
                (cols_hbm, cols_ref),
                (coeff_hbm, coeff_ref),
            ]
        )
    ]
    entries[0].start()
    entries[1].start()

    def halo_target(which):
        return lax.rem(me + shift_amount(which) + n, n)

    def group_mate(k):
        return me // GROUP * GROUP + lax.rem(lax.rem(me, GROUP) + k, GROUP)

    def other_group(k):
        return lax.rem(me + k * GROUP, n)

    barrier = pltpu.get_barrier_semaphore()
    partners = [halo_target(w) for w in range(neighbours)]
    partners += [group_mate(k) for k in range(1, GROUP)]
    partners += [other_group(k) for k in range(1, groups)]
    for partner in partners:
        pl.semaphore_signal(barrier, inc=1, device_id=(partner,), device_id_type=MESH)

    prev_copy = pltpu.make_async_copy(prev_hbm, prev, prev_sem)

    def tile_copy(c):
        piece = pl.ds(c * size, size)
        return pltpu.make_async_copy(tiles_hbm.at[piece], tiles.at[piece], tile_sem.at[c])

    for copy in entries[2:]:
        copy.start()

    def gather(step, half, which):
        base = ((step * 2 + half) * neighbours + which) * count
        for s in range(count):
            index = sends_ref[which, 0, s]
            if step == 0:
                outgoing[base + s] = (start_b if half else start_a)[index]
            else:
                outgoing[base + s] = own[step][half][index]

    def halo_copy(step, half, which):
        slot = (step * 2 + half) * neighbours + which
        return pltpu.make_async_remote_copy(
            src_ref=outgoing.at[pl.ds(slot * count, count)],
            dst_ref=ext[step][half].at[pl.ds(capacity + which * count, count)],
            send_sem=halo_send.at[step * 2 + half],
            recv_sem=halo_recv.at[step * 2 + half],
            device_id=(halo_target(which),),
            device_id_type=MESH,
        )

    def halo_whole(step, half):
        ghosts = neighbours * count
        return pltpu.make_async_remote_copy(
            src_ref=outgoing.at[pl.ds((step * 2 + half) * ghosts, ghosts)],
            dst_ref=ext[step][half].at[pl.ds(capacity, ghosts)],
            send_sem=halo_send.at[step * 2 + half],
            recv_sem=halo_recv.at[step * 2 + half],
            device_id=(halo_target(0),),
            device_id_type=MESH,
        )

    order = (4, 5, 2, 3, 0, 1)
    entries[0].wait()
    entries[1].wait()
    prev_copy.start()
    tile_copy(0).start()
    for which in order:
        gather(0, 0, which)
    pl.semaphore_wait(barrier, len(partners))
    for which in order:
        halo_copy(0, 0, which).start()
    entries[2].wait()
    for which in order:
        gather(0, 1, which)

    for copy in entries[3:]:
        copy.wait()
    live = live_ref[0]

    def mask(b):
        return jnp.where(b < live, 1.0, 0.0).astype(F32)

    def fill(b, carry):
        ext_a0[b] = (start_a[b].astype(F32) * mask(b)).astype(BF16)
        ext_b0[b] = (start_b[b].astype(F32) * mask(b)).astype(BF16)
        return carry

    lax.fori_loop(0, capacity, fill, 0, unroll=4)

    def within_copy(which, k):
        return pltpu.make_async_remote_copy(
            src_ref=mine.at[2 * which],
            dst_ref=within.at[which * (GROUP - 1) + k - 1],
            send_sem=sum_send.at[2 * which],
            recv_sem=sum_recv.at[2 * which],
            device_id=(group_mate(k),),
            device_id_type=MESH,
        )

    def across_copy(which, k):
        return pltpu.make_async_remote_copy(
            src_ref=mine.at[2 * which + 1],
            dst_ref=across.at[which * (groups - 1) + k - 1],
            send_sem=sum_send.at[2 * which + 1],
            recv_sem=sum_recv.at[2 * which + 1],
            device_id=(other_group(k),),
            device_id_type=MESH,
        )

    def sum_whole(which, landing):
        peers = landing.shape[0] // 2
        slot = 2 * which + (0 if landing is within else 1)
        return pltpu.make_async_remote_copy(
            src_ref=landing.at[pl.ds(which * peers, peers)],
            dst_ref=landing.at[pl.ds(which * peers, peers)],
            send_sem=sum_send.at[slot],
            recv_sem=sum_recv.at[slot],
            device_id=(group_mate(1),),
            device_id_type=MESH,
        )

    def sum_start(which, value):
        mine[2 * which] = value
        for k in range(1, GROUP):
            within_copy(which, k).start()

    def sum_middle(which):
        total = mine[2 * which]
        sum_whole(which, within).wait_recv()
        for k in range(1, GROUP):
            total += within[which * (GROUP - 1) + k - 1]
        mine[2 * which + 1] = total
        for k in range(1, groups):
            across_copy(which, k).start()

    def sum_end(which):
        total = mine[2 * which + 1]
        sum_whole(which, across).wait_recv()
        for k in range(1, groups):
            total += across[which * (groups - 1) + k - 1]
        return total

    prev_copy.wait()
    for c in range(1, CHUNKS):
        tile_copy(c).start()

    def prev_gram(pair, total):
        left, right = [], []
        for b in (2 * pair, 2 * pair + 1):
            high, low = split(prev[b] * mask(b))
            y_high[b, :32] = high
            y_low[b, :32] = low
            left.append(jnp.concatenate([high, low], axis=0))
            right.append(jnp.concatenate([high, high, low, low], axis=0))
        return total + rows_dot(
            jnp.concatenate(left, axis=1), jnp.concatenate(right, axis=1)
        )

    total = lax.fori_loop(0, capacity // 2, prev_gram, jnp.zeros((64, 128), F32), unroll=2)
    sum_start(0, pack(total[:32] + total[32:]))
    halo_whole(0, 0).wait_send()
    for which in order:
        halo_copy(0, 1, which).start()

    def product(step, half, b):
        vectors = ext[step][half]
        picked = jnp.concatenate([vectors[cols_ref[k, b]] for k in range(fan)], axis=1)
        return jnp.dot(picked, tiles[b], preferred_element_type=F32) * mask(b)

    c0, c1, c2, c3 = (coeff_ref[i] for i in range(4))

    def first_step(half, b):
        result = product(0, half, b)
        rounded = result.astype(BF16)
        first[half, b] = result
        own[1][half][b] = rounded
        ext[1][half][b] = rounded

    def second_step(half, b):
        before = ext[0][half][b].astype(F32)
        one = first[half, b]
        result = 2.0 * product(1, half, b) - before
        rounded = result.astype(BF16)
        own[2][half][b] = rounded
        ext[2][half][b] = rounded
        accum[half, b] = c0 * before + (c1 - c3) * one + c2 * result

    def third_step(half, b):
        rows = slice(32 + 16 * half, 48 + 16 * half)
        high, low = split(accum[half, b] + (2.0 * c3) * product(2, half, b))
        y_high[b, rows] = high
        y_low[b, rows] = low

    def await_halo(step, half):
        halo_whole(step, half).wait_recv()

    def loop(body, lower, upper):
        def one(b, carry):
            body(b)
            return carry

        lax.fori_loop(lower, upper, one, 0, unroll=BLOCKS)

    for half in range(2):
        await_halo(0, half)
        if half == 0:
            for c in range(CHUNKS):
                tile_copy(c).wait()
        loop(functools.partial(first_step, half), 0, capacity)
        for which in order:
            gather(1, half, which)
        if half == 0:
            halo_whole(0, 1).wait_send()
        for which in order:
            halo_copy(1, half, which).start()
        if half == 0:
            sum_middle(0)

    rows, lanes = iota(0), iota(1)
    gram = unpack(sum_end(0))
    matrix = jnp.where(lanes < 32, gram, jnp.where(lanes == rows + 64, 1.0, 0.0))
    matrix, diagonal = eliminate(matrix, True)
    middle = (lanes >= 32) & (lanes < 64)
    state_ref[:32] = jnp.where(middle, pltpu.roll(matrix / diagonal, 96, 1), 0.0)

    for half in range(2):
        await_halo(1, half)
        loop(functools.partial(second_step, half), 0, capacity)
        for which in order:
            gather(2, half, which)
            halo_copy(2, half, which).start()

    await_halo(2, 0)
    def third_group(half, group):
        for i in range(SPAN):
            third_step(half, group * SPAN + i)

    def filtered_gram(group, total):
        for i in range(0, SPAN, 2):
            left, right = [], []
            for b in (group * SPAN + i, group * SPAN + i + 1):
                left.append(jnp.concatenate([y_high[b, 32:64], y_low[b, 32:64]], axis=0))
                right.append(jnp.concatenate([y_high[b], y_low[b]], axis=0))
            total += rows_dot(
                jnp.concatenate(left, axis=1), jnp.concatenate(right, axis=1)
            )
        return total

    def last_group(group, total):
        total = filtered_gram(group - 1, total)
        third_group(1, group)
        return total

    loop(functools.partial(third_step, 0), 0, capacity)
    await_halo(2, 1)
    third_group(1, 0)
    total = lax.fori_loop(1, capacity // SPAN, last_group, jnp.zeros((64, 128), F32))
    total = filtered_gram(capacity // SPAN - 1, total)
    out_copies = [
        pltpu.make_async_copy(y_high, high_hbm, out_sem.at[0]),
        pltpu.make_async_copy(y_low, low_hbm, out_sem.at[1]),
    ]
    sum_start(1, pack(total[:32] + total[32:]))
    for copy in out_copies:
        copy.start()
    sum_middle(1)
    state_ref[32:] = unpack(sum_end(1))
    for copy in out_copies:
        copy.wait()
    for step in range(1, 3):
        for half in range(2):
            halo_whole(step, half).wait_send()
    for which in range(2):
        sum_whole(which, within).wait_send()
        sum_whole(which, across).wait_send()


def finish(
    scale, state_hbm, high_hbm, low_hbm, out_hbm, state, high, low, out,
    state_sem, in_sem, out_sem,
):
    size = high.shape[0] // PARTS
    pieces = [pl.ds(c * size, size) for c in range(PARTS)]
    reads = [
        [
            pltpu.make_async_copy(high_hbm.at[piece], high.at[piece], in_sem.at[0, c]),
            pltpu.make_async_copy(low_hbm.at[piece], low.at[piece], in_sem.at[1, c]),
        ]
        for c, piece in enumerate(pieces)
    ]
    writes = [
        pltpu.make_async_copy(out.at[piece], out_hbm.at[piece], out_sem.at[c])
        for c, piece in enumerate(pieces)
    ]
    state_copy = pltpu.make_async_copy(state_hbm, state, state_sem)
    state_copy.start()
    state_copy.wait()
    for pair in reads:
        for copy in pair:
            copy.start()
    factor = solve(scale, state[...])
    for c in range(PARTS):
        for copy in reads[c]:
            copy.wait()
        for b in range(c * size, (c + 1) * size, 2):
            stacked = [
                jnp.concatenate([high[i], high[i], low[i], low[i]], axis=0) for i in (b, b + 1)
            ]
            result = jnp.dot(
                factor, jnp.concatenate(stacked, axis=1), preferred_element_type=F32
            )
            out[b] = result[:, :128]
            out[b + 1] = result[:, 128:]
        writes[c].start()
    for copy in writes:
        copy.wait()


def shards(
    live_blocks, tile_columns, send_lists, tiles, filter_coeffs, start_block, previous_block
):
    n = lax.axis_size("rows")
    capacity, vectors, rows = start_block.shape
    fan = tile_columns.shape[1]
    _, neighbours, count = send_lists.shape
    groups = n // GROUP
    vmem = pl.BlockSpec(memory_space=pltpu.VMEM)
    hbm = pl.BlockSpec(memory_space=pl.ANY)
    half = vectors // 2
    field = pltpu.VMEM((capacity, half, rows), BF16)
    extended = pltpu.VMEM((capacity + neighbours * count, half, rows), BF16)
    wide = pltpu.VMEM((2, capacity, half, rows), F32)
    stacked = pltpu.VMEM((capacity, 2 * vectors, rows), BF16)
    scale = math.sqrt(capacity * n * rows)
    state, high, low = pl.pallas_call(
        functools.partial(kernel, n),
        out_shape=[jax.ShapeDtypeStruct((2 * vectors, 128), F32)]
        + [jax.ShapeDtypeStruct((capacity, 2 * vectors, rows), BF16)] * 2,
        in_specs=[hbm] * 7,
        out_specs=[vmem, hbm, hbm],
        scratch_shapes=[
            pltpu.SMEM(live_blocks.shape, jnp.int32),
            pltpu.SMEM((fan, capacity), jnp.int32),
            pltpu.SMEM((neighbours, 1, count), jnp.int32),
            pltpu.SMEM(filter_coeffs.shape, F32),
            field,
            field,
            pltpu.VMEM((capacity, fan * rows, rows), BF16),
            pltpu.VMEM((capacity, vectors, rows), F32),
            *[extended] * 6,
            *[field] * 4,
            pltpu.VMEM((6 * neighbours * count, half, rows), BF16),
            wide,
            wide,
            stacked,
            stacked,
            pltpu.VMEM((4, 16, 128), F32),
            pltpu.VMEM((2 * (GROUP - 1), 16, 128), F32),
            pltpu.VMEM((2 * (groups - 1), 16, 128), F32),
            pltpu.SemaphoreType.DMA((6,)),
            pltpu.SemaphoreType.DMA((CHUNKS,)),
            pltpu.SemaphoreType.DMA,
            pltpu.SemaphoreType.DMA((2,)),
            pltpu.SemaphoreType.DMA((6,)),
            pltpu.SemaphoreType.DMA((6,)),
            pltpu.SemaphoreType.DMA((4,)),
            pltpu.SemaphoreType.DMA((4,)),
        ],
        compiler_params=pltpu.CompilerParams(
            collective_id=0, has_side_effects=True, vmem_limit_bytes=64 * 1024 * 1024
        ),
        name="filtered_step",
    )(
        live_blocks,
        tile_columns.T,
        jnp.transpose(send_lists, (1, 0, 2)),
        filter_coeffs,
        start_block,
        tiles.reshape(capacity, fan * rows, rows),
        previous_block,
    )
    return pl.pallas_call(
        functools.partial(finish, scale),
        out_shape=jax.ShapeDtypeStruct((capacity, vectors, rows), F32),
        in_specs=[hbm, hbm, hbm],
        out_specs=hbm,
        scratch_shapes=[
            pltpu.VMEM((2 * vectors, 128), F32),
            stacked,
            stacked,
            pltpu.VMEM((capacity, vectors, rows), F32),
            pltpu.SemaphoreType.DMA,
            pltpu.SemaphoreType.DMA((2, PARTS)),
            pltpu.SemaphoreType.DMA((PARTS,)),
        ],
        compiler_params=pltpu.CompilerParams(vmem_limit_bytes=64 * 1024 * 1024),
        name="finish",
    )(state, high, low)


def solution(mesh):
    return jax.shard_map(
        shards,
        mesh=mesh,
        in_specs=(
            P("rows"),
            P("rows", None),
            P("rows", None, None),
            P("rows", None, None, None),
            P(),
            P("rows", None, None),
            P("rows", None, None),
        ),
        out_specs=P("rows", None, None),
        check_vma=False,
    )
```

```python
import functools
import math

import jax
import jax.numpy as jnp
from jax import lax
from jax.experimental import pallas as pl
from jax.experimental.pallas import tpu as pltpu
from jax.sharding import PartitionSpec as P

MESH = pl.DeviceIdType.MESH
HIGHEST = lax.Precision.HIGHEST
GROUP = 8
PIVOTS = 8
PARTS = 3
BLOCKS = 24
SPAN = 24
CHUNKS = 8
F32, BF16 = jnp.float32, jnp.bfloat16

rows_dot = functools.partial(
    lax.dot_general, dimension_numbers=(((1,), (1,)), ((), ())), preferred_element_type=F32
)


def shift_amount(which):
    return (which // 2 + 1) * (1 if which % 2 == 0 else -1)


def iota(axis):
    return lax.broadcasted_iota(jnp.int32, (32, 128), axis)


def split(value):
    high = value.astype(BF16)
    return high, (value - high.astype(F32)).astype(BF16)


def eliminate(matrix, full):
    rows = iota(0)
    diagonal = jnp.zeros((32, 128), F32)
    for start in range(0, 32, PIVOTS):
        columns = [
            jnp.broadcast_to(matrix[:, j : j + 1], (32, 128))
            for j in range(start, start + PIVOTS)
        ]
        for p in range(PIVOTS):
            j = start + p
            row, column = matrix[j : j + 1, :], columns[p]
            keep = (rows != j) if full else (rows > j)
            factor = jnp.where(keep, column * (1.0 / column[j : j + 1, :]), 0.0)
            diagonal = jnp.where(rows == j, column, diagonal)
            matrix = matrix - factor * row
            for q in range(p + 1, PIVOTS):
                columns[q] = columns[q] - factor * columns[q][j : j + 1, :]
    return matrix, diagonal


def pack(total):
    folded = total + pltpu.roll(total, 64, 1)
    return jnp.where(iota(1)[:16] < 64, folded[:16], folded[16:])


def unpack(packed):
    return jnp.concatenate([packed, pltpu.roll(packed, 64, 1)], axis=0)


def solve(scale, state):
    rows, lanes = iota(0), iota(1)
    sums = state[32:]
    cross = jnp.where(lanes < 32, sums, 0.0)
    below = jnp.zeros((96, 128), F32)
    coeff = jnp.dot(
        cross, jnp.concatenate([state[:32], below], axis=0),
        precision=HIGHEST, preferred_element_type=F32,
    )
    removed = rows_dot(
        coeff, jnp.concatenate([pltpu.roll(cross, 32, 1), below], axis=0), precision=HIGHEST
    )
    matrix = jnp.where(
        lanes < 32,
        pltpu.roll(sums, 96, 1) - removed,
        jnp.where(lanes < 64, -coeff, jnp.where(lanes == rows + 64, 1.0, 0.0)),
    )
    matrix, diagonal = eliminate(matrix, False)
    factor = pltpu.roll(matrix * (scale * lax.rsqrt(diagonal)), 96, 1)
    factor = jnp.where(lanes < 64, factor, 0.0)
    high = factor.astype(BF16).astype(F32)
    both = jnp.where(lanes < 64, high, pltpu.roll(factor - high, 64, 1)).astype(BF16)
    return jnp.concatenate([both, both], axis=1)


def kernel(
    n, live_hbm, cols_hbm, sends_hbm, coeff_hbm, start_hbm, tiles_hbm, prev_hbm,
    state_ref, high_hbm, low_hbm,
    live_ref, cols_ref, sends_ref, coeff_ref, start_a, start_b, tiles, prev, ext_a0, ext_b0, ext_a1, ext_b1, ext_a2, ext_b2, own_a1, own_b1, own_a2, own_b2,
    outgoing, first, accum, y_high, y_low, mine, within, across,
    entry_sem, tile_sem, prev_sem, out_sem, halo_send, halo_recv, sum_send, sum_recv,
):
    capacity = start_a.shape[0]
    fan = cols_ref.shape[0]
    size = capacity // CHUNKS
    neighbours, _, count = sends_ref.shape
    groups = n // GROUP
    me = lax.axis_index("rows")
    ext = [[ext_a0, ext_b0], [ext_a1, ext_b1], [ext_a2, ext_b2]]
    own = [None, [own_a1, own_b1], [own_a2, own_b2]]
    def entry_copy(source, target, which):
        return pltpu.make_async_copy(source, target, entry_sem.at[which])

    entries = [
        entry_copy(*pair, i)
        for i, pair in enumerate(
            [
                (sends_hbm, sends_ref),
                (start_hbm.at[:, :16], start_a),
                (start_hbm.at[:, 16:], start_b),
                (live_hbm, live_ref),
                (cols_hbm, cols_ref),
                (coeff_hbm, coeff_ref),
            ]
        )
    ]
    entries[0].start()
    entries[1].start()

    def halo_target(which):
        return lax.rem(me + shift_amount(which) + n, n)

    def group_mate(k):
        return me // GROUP * GROUP + lax.rem(lax.rem(me, GROUP) + k, GROUP)

    def other_group(k):
        return lax.rem(me + k * GROUP, n)

    barrier = pltpu.get_barrier_semaphore()
    partners = [halo_target(w) for w in range(neighbours)]
    partners += [group_mate(k) for k in range(1, GROUP)]
    partners += [other_group(k) for k in range(1, groups)]
    for partner in partners:
        pl.semaphore_signal(barrier, inc=1, device_id=(partner,), device_id_type=MESH)

    prev_copy = pltpu.make_async_copy(prev_hbm, prev, prev_sem)

    def tile_copy(c):
        piece = pl.ds(c * size, size)
        return pltpu.make_async_copy(tiles_hbm.at[piece], tiles.at[piece], tile_sem.at[c])

    for copy in entries[2:]:
        copy.start()

    def gather(step, half, which):
        base = ((step * 2 + half) * neighbours + which) * count
        for s in range(count):
            index = sends_ref[which, 0, s]
            if step == 0:
                outgoing[base + s] = (start_b if half else start_a)[index]
            else:
                outgoing[base + s] = own[step][half][index]

    def halo_copy(step, half, which):
        slot = (step * 2 + half) * neighbours + which
        return pltpu.make_async_remote_copy(
            src_ref=outgoing.at[pl.ds(slot * count, count)],
            dst_ref=ext[step][half].at[pl.ds(capacity + which * count, count)],
            send_sem=halo_send.at[step * 2 + half],
            recv_sem=halo_recv.at[step * 2 + half],
            device_id=(halo_target(which),),
            device_id_type=MESH,
        )

    def halo_whole(step, half):
        ghosts = neighbours * count
        return pltpu.make_async_remote_copy(
            src_ref=outgoing.at[pl.ds((step * 2 + half) * ghosts, ghosts)],
            dst_ref=ext[step][half].at[pl.ds(capacity, ghosts)],
            send_sem=halo_send.at[step * 2 + half],
            recv_sem=halo_recv.at[step * 2 + half],
            device_id=(halo_target(0),),
            device_id_type=MESH,
        )

    order = (4, 5, 2, 3, 0, 1)
    entries[0].wait()
    entries[1].wait()
    prev_copy.start()
    tile_copy(0).start()
    for which in order:
        gather(0, 0, which)
    pl.semaphore_wait(barrier, len(partners))
    for which in order:
        halo_copy(0, 0, which).start()
    entries[2].wait()
    for which in order:
        gather(0, 1, which)

    for copy in entries[3:]:
        copy.wait()
    live = live_ref[0]

    def mask(b):
        return jnp.where(b < live, 1.0, 0.0).astype(F32)

    def fill(b, carry):
        ext_a0[b] = (start_a[b].astype(F32) * mask(b)).astype(BF16)
        ext_b0[b] = (start_b[b].astype(F32) * mask(b)).astype(BF16)
        return carry

    lax.fori_loop(0, capacity, fill, 0, unroll=4)

    def within_copy(which, k):
        return pltpu.make_async_remote_copy(
            src_ref=mine.at[2 * which],
            dst_ref=within.at[which * (GROUP - 1) + k - 1],
            send_sem=sum_send.at[2 * which],
            recv_sem=sum_recv.at[2 * which],
            device_id=(group_mate(k),),
            device_id_type=MESH,
        )

    def across_copy(which, k):
        return pltpu.make_async_remote_copy(
            src_ref=mine.at[2 * which + 1],
            dst_ref=across.at[which * (groups - 1) + k - 1],
            send_sem=sum_send.at[2 * which + 1],
            recv_sem=sum_recv.at[2 * which + 1],
            device_id=(other_group(k),),
            device_id_type=MESH,
        )

    def sum_whole(which, landing):
        peers = landing.shape[0] // 2
        slot = 2 * which + (0 if landing is within else 1)
        return pltpu.make_async_remote_copy(
            src_ref=landing.at[pl.ds(which * peers, peers)],
            dst_ref=landing.at[pl.ds(which * peers, peers)],
            send_sem=sum_send.at[slot],
            recv_sem=sum_recv.at[slot],
            device_id=(group_mate(1),),
            device_id_type=MESH,
        )

    def sum_start(which, value):
        mine[2 * which] = value
        for k in range(1, GROUP):
            within_copy(which, k).start()

    def sum_middle(which):
        total = mine[2 * which]
        sum_whole(which, within).wait_recv()
        for k in range(1, GROUP):
            total += within[which * (GROUP - 1) + k - 1]
        mine[2 * which + 1] = total
        for k in range(1, groups):
            across_copy(which, k).start()

    def sum_end(which):
        total = mine[2 * which + 1]
        sum_whole(which, across).wait_recv()
        for k in range(1, groups):
            total += across[which * (groups - 1) + k - 1]
        return total

    prev_copy.wait()
    for c in range(1, CHUNKS):
        tile_copy(c).start()

    def prev_gram(pair, total):
        left, right = [], []
        for b in (2 * pair, 2 * pair + 1):
            high, low = split(prev[b] * mask(b))
            y_high[b, :32] = high
            y_low[b, :32] = low
            left.append(jnp.concatenate([high, low], axis=0))
            right.append(jnp.concatenate([high, high, low, low], axis=0))
        return total + rows_dot(
            jnp.concatenate(left, axis=1), jnp.concatenate(right, axis=1)
        )

    total = lax.fori_loop(0, capacity // 2, prev_gram, jnp.zeros((64, 128), F32), unroll=2)
    sum_start(0, pack(total[:32] + total[32:]))
    halo_whole(0, 0).wait_send()
    for which in order:
        halo_copy(0, 1, which).start()

    def product(step, half, b):
        vectors = ext[step][half]
        picked = jnp.concatenate([vectors[cols_ref[k, b]] for k in range(fan)], axis=1)
        return jnp.dot(picked, tiles[b], preferred_element_type=F32) * mask(b)

    c0, c1, c2, c3 = (coeff_ref[i] for i in range(4))

    def first_step(half, b):
        result = product(0, half, b)
        rounded = result.astype(BF16)
        first[half, b] = result
        own[1][half][b] = rounded
        ext[1][half][b] = rounded

    def second_step(half, b):
        before = ext[0][half][b].astype(F32)
        one = first[half, b]
        result = 2.0 * product(1, half, b) - before
        rounded = result.astype(BF16)
        own[2][half][b] = rounded
        ext[2][half][b] = rounded
        accum[half, b] = c0 * before + (c1 - c3) * one + c2 * result

    def third_step(half, b):
        rows = slice(32 + 16 * half, 48 + 16 * half)
        high, low = split(accum[half, b] + (2.0 * c3) * product(2, half, b))
        y_high[b, rows] = high
        y_low[b, rows] = low

    def await_halo(step, half):
        halo_whole(step, half).wait_recv()

    def loop(body, lower, upper):
        def one(b, carry):
            body(b)
            return carry

        lax.fori_loop(lower, upper, one, 0, unroll=BLOCKS)

    for half in range(2):
        await_halo(0, half)
        if half == 0:
            for c in range(CHUNKS):
                tile_copy(c).wait()
        loop(functools.partial(first_step, half), 0, capacity)
        for which in order:
            gather(1, half, which)
        if half == 0:
            halo_whole(0, 1).wait_send()
        for which in order:
            halo_copy(1, half, which).start()
        if half == 0:
            sum_middle(0)

    rows, lanes = iota(0), iota(1)
    gram = unpack(sum_end(0))
    matrix = jnp.where(lanes < 32, gram, jnp.where(lanes == rows + 64, 1.0, 0.0))
    matrix, diagonal = eliminate(matrix, True)
    middle = (lanes >= 32) & (lanes < 64)
    state_ref[:32] = jnp.where(middle, pltpu.roll(matrix / diagonal, 96, 1), 0.0)

    for half in range(2):
        await_halo(1, half)
        loop(functools.partial(second_step, half), 0, capacity)
        for which in order:
            gather(2, half, which)
            halo_copy(2, half, which).start()

    await_halo(2, 0)
    def third_group(half, group):
        for i in range(SPAN):
            third_step(half, group * SPAN + i)

    def filtered_gram(group, total):
        for i in range(0, SPAN, 2):
            left, right = [], []
            for b in (group * SPAN + i, group * SPAN + i + 1):
                left.append(jnp.concatenate([y_high[b, 32:64], y_low[b, 32:64]], axis=0))
                right.append(jnp.concatenate([y_high[b], y_low[b]], axis=0))
            total += rows_dot(
                jnp.concatenate(left, axis=1), jnp.concatenate(right, axis=1)
            )
        return total

    def last_group(group, total):
        total = filtered_gram(group - 1, total)
        third_group(1, group)
        return total

    loop(functools.partial(third_step, 0), 0, capacity)
    await_halo(2, 1)
    third_group(1, 0)
    total = lax.fori_loop(1, capacity // SPAN, last_group, jnp.zeros((64, 128), F32))
    total = filtered_gram(capacity // SPAN - 1, total)
    out_copies = [
        pltpu.make_async_copy(y_high, high_hbm, out_sem.at[0]),
        pltpu.make_async_copy(y_low, low_hbm, out_sem.at[1]),
    ]
    sum_start(1, pack(total[:32] + total[32:]))
    for copy in out_copies:
        copy.start()
    sum_middle(1)
    state_ref[32:] = unpack(sum_end(1))
    for copy in out_copies:
        copy.wait()
    for step in range(1, 3):
        for half in range(2):
            halo_whole(step, half).wait_send()
    for which in range(2):
        sum_whole(which, within).wait_send()
        sum_whole(which, across).wait_send()


def finish(
    scale, state_hbm, high_hbm, low_hbm, out_hbm, state, high, low, out,
    state_sem, in_sem, out_sem,
):
    size = high.shape[0] // PARTS
    pieces = [pl.ds(c * size, size) for c in range(PARTS)]
    reads = [
        [
            pltpu.make_async_copy(high_hbm.at[piece], high.at[piece], in_sem.at[0, c]),
            pltpu.make_async_copy(low_hbm.at[piece], low.at[piece], in_sem.at[1, c]),
        ]
        for c, piece in enumerate(pieces)
    ]
    writes = [
        pltpu.make_async_copy(out.at[piece], out_hbm.at[piece], out_sem.at[c])
        for c, piece in enumerate(pieces)
    ]
    state_copy = pltpu.make_async_copy(state_hbm, state, state_sem)
    state_copy.start()
    for pair in reads:
        for copy in pair:
            copy.start()
    state_copy.wait()
    factor = solve(scale, state[...])
    for c in range(PARTS):
        for copy in reads[c]:
            copy.wait()
        for b in range(c * size, (c + 1) * size, 2):
            stacked = [
                jnp.concatenate([high[i], high[i], low[i], low[i]], axis=0) for i in (b, b + 1)
            ]
            result = jnp.dot(
                factor, jnp.concatenate(stacked, axis=1), preferred_element_type=F32
            )
            out[b] = result[:, :128]
            out[b + 1] = result[:, 128:]
        writes[c].start()
    for copy in writes:
        copy.wait()


def shards(
    live_blocks, tile_columns, send_lists, tiles, filter_coeffs, start_block, previous_block
):
    n = lax.axis_size("rows")
    capacity, vectors, rows = start_block.shape
    fan = tile_columns.shape[1]
    _, neighbours, count = send_lists.shape
    groups = n // GROUP
    vmem = pl.BlockSpec(memory_space=pltpu.VMEM)
    hbm = pl.BlockSpec(memory_space=pl.ANY)
    half = vectors // 2
    field = pltpu.VMEM((capacity, half, rows), BF16)
    extended = pltpu.VMEM((capacity + neighbours * count, half, rows), BF16)
    wide = pltpu.VMEM((2, capacity, half, rows), F32)
    stacked = pltpu.VMEM((capacity, 2 * vectors, rows), BF16)
    scale = math.sqrt(capacity * n * rows)
    state, high, low = pl.pallas_call(
        functools.partial(kernel, n),
        out_shape=[jax.ShapeDtypeStruct((2 * vectors, 128), F32)]
        + [jax.ShapeDtypeStruct((capacity, 2 * vectors, rows), BF16)] * 2,
        in_specs=[hbm] * 7,
        out_specs=[vmem, hbm, hbm],
        scratch_shapes=[
            pltpu.SMEM(live_blocks.shape, jnp.int32),
            pltpu.SMEM((fan, capacity), jnp.int32),
            pltpu.SMEM((neighbours, 1, count), jnp.int32),
            pltpu.SMEM(filter_coeffs.shape, F32),
            field,
            field,
            pltpu.VMEM((capacity, fan * rows, rows), BF16),
            pltpu.VMEM((capacity, vectors, rows), F32),
            *[extended] * 6,
            *[field] * 4,
            pltpu.VMEM((6 * neighbours * count, half, rows), BF16),
            wide,
            wide,
            stacked,
            stacked,
            pltpu.VMEM((4, 16, 128), F32),
            pltpu.VMEM((2 * (GROUP - 1), 16, 128), F32),
            pltpu.VMEM((2 * (groups - 1), 16, 128), F32),
            pltpu.SemaphoreType.DMA((6,)),
            pltpu.SemaphoreType.DMA((CHUNKS,)),
            pltpu.SemaphoreType.DMA,
            pltpu.SemaphoreType.DMA((2,)),
            pltpu.SemaphoreType.DMA((6,)),
            pltpu.SemaphoreType.DMA((6,)),
            pltpu.SemaphoreType.DMA((4,)),
            pltpu.SemaphoreType.DMA((4,)),
        ],
        compiler_params=pltpu.CompilerParams(
            collective_id=0, has_side_effects=True, vmem_limit_bytes=64 * 1024 * 1024
        ),
        name="filtered_step",
    )(
        live_blocks,
        tile_columns.T,
        jnp.transpose(send_lists, (1, 0, 2)),
        filter_coeffs,
        start_block,
        tiles.reshape(capacity, fan * rows, rows),
        previous_block,
    )
    return pl.pallas_call(
        functools.partial(finish, scale),
        out_shape=jax.ShapeDtypeStruct((capacity, vectors, rows), F32),
        in_specs=[hbm, hbm, hbm],
        out_specs=hbm,
        scratch_shapes=[
            pltpu.VMEM((2 * vectors, 128), F32),
            stacked,
            stacked,
            pltpu.VMEM((capacity, vectors, rows), F32),
            pltpu.SemaphoreType.DMA,
            pltpu.SemaphoreType.DMA((2, PARTS)),
            pltpu.SemaphoreType.DMA((PARTS,)),
        ],
        compiler_params=pltpu.CompilerParams(vmem_limit_bytes=64 * 1024 * 1024),
        name="finish",
    )(state, high, low)


def solution(mesh):
    return jax.shard_map(
        shards,
        mesh=mesh,
        in_specs=(
            P("rows"),
            P("rows", None),
            P("rows", None, None),
            P("rows", None, None, None),
            P(),
            P("rows", None, None),
            P("rows", None, None),
        ),
        out_specs=P("rows", None, None),
        check_vma=False,
    )
```

```python
import functools
import math

import jax
import jax.numpy as jnp
from jax import lax
from jax.experimental import pallas as pl
from jax.experimental.pallas import tpu as pltpu
from jax.sharding import PartitionSpec as P

MESH = pl.DeviceIdType.MESH
HIGHEST = lax.Precision.HIGHEST
GROUP = 8
PIVOTS = 16
PARTS = 3
BLOCKS = 24
SPAN = 24
CHUNKS = 8
F32, BF16 = jnp.float32, jnp.bfloat16

rows_dot = functools.partial(
    lax.dot_general, dimension_numbers=(((1,), (1,)), ((), ())), preferred_element_type=F32
)


def shift_amount(which):
    return (which // 2 + 1) * (1 if which % 2 == 0 else -1)


def iota(axis):
    return lax.broadcasted_iota(jnp.int32, (32, 128), axis)


def split(value):
    high = value.astype(BF16)
    return high, (value - high.astype(F32)).astype(BF16)


def eliminate(matrix, full):
    rows = iota(0)
    diagonal = jnp.zeros((32, 128), F32)
    for start in range(0, 32, PIVOTS):
        columns = [
            jnp.broadcast_to(matrix[:, j : j + 1], (32, 128))
            for j in range(start, start + PIVOTS)
        ]
        for p in range(PIVOTS):
            j = start + p
            row, column = matrix[j : j + 1, :], columns[p]
            keep = (rows != j) if full else (rows > j)
            factor = jnp.where(keep, column * (1.0 / column[j : j + 1, :]), 0.0)
            diagonal = jnp.where(rows == j, column, diagonal)
            matrix = matrix - factor * row
            for q in range(p + 1, PIVOTS):
                columns[q] = columns[q] - factor * columns[q][j : j + 1, :]
    return matrix, diagonal


def pack(total):
    folded = total + pltpu.roll(total, 64, 1)
    return jnp.where(iota(1)[:16] < 64, folded[:16], folded[16:])


def unpack(packed):
    return jnp.concatenate([packed, pltpu.roll(packed, 64, 1)], axis=0)


def solve(scale, state):
    rows, lanes = iota(0), iota(1)
    sums = state[32:]
    cross = jnp.where(lanes < 32, sums, 0.0)
    below = jnp.zeros((96, 128), F32)
    coeff = jnp.dot(
        cross, jnp.concatenate([state[:32], below], axis=0),
        precision=HIGHEST, preferred_element_type=F32,
    )
    removed = rows_dot(
        coeff, jnp.concatenate([pltpu.roll(cross, 32, 1), below], axis=0), precision=HIGHEST
    )
    matrix = jnp.where(
        lanes < 32,
        pltpu.roll(sums, 96, 1) - removed,
        jnp.where(lanes < 64, -coeff, jnp.where(lanes == rows + 64, 1.0, 0.0)),
    )
    matrix, diagonal = eliminate(matrix, False)
    factor = pltpu.roll(matrix * (scale * lax.rsqrt(diagonal)), 96, 1)
    factor = jnp.where(lanes < 64, factor, 0.0)
    high = factor.astype(BF16).astype(F32)
    both = jnp.where(lanes < 64, high, pltpu.roll(factor - high, 64, 1)).astype(BF16)
    return jnp.concatenate([both, both], axis=1)


def kernel(
    n, live_hbm, cols_hbm, sends_hbm, coeff_hbm, start_hbm, tiles_hbm, prev_hbm,
    state_ref, high_hbm, low_hbm,
    live_ref, cols_ref, sends_ref, coeff_ref, start_a, start_b, tiles, prev, ext_a0, ext_b0, ext_a1, ext_b1, ext_a2, ext_b2, own_a1, own_b1, own_a2, own_b2,
    outgoing, first, accum, y_high, y_low, mine, within, across,
    entry_sem, tile_sem, prev_sem, out_sem, halo_send, halo_recv, sum_send, sum_recv,
):
    capacity = start_a.shape[0]
    fan = cols_ref.shape[0]
    size = capacity // CHUNKS
    neighbours, _, count = sends_ref.shape
    groups = n // GROUP
    me = lax.axis_index("rows")
    ext = [[ext_a0, ext_b0], [ext_a1, ext_b1], [ext_a2, ext_b2]]
    own = [None, [own_a1, own_b1], [own_a2, own_b2]]
    def entry_copy(source, target, which):
        return pltpu.make_async_copy(source, target, entry_sem.at[which])

    entries = [
        entry_copy(*pair, i)
        for i, pair in enumerate(
            [
                (sends_hbm, sends_ref),
                (start_hbm.at[:, :16], start_a),
                (start_hbm.at[:, 16:], start_b),
                (live_hbm, live_ref),
                (cols_hbm, cols_ref),
                (coeff_hbm, coeff_ref),
            ]
        )
    ]
    entries[0].start()
    entries[1].start()

    def halo_target(which):
        return lax.rem(me + shift_amount(which) + n, n)

    def group_mate(k):
        return me // GROUP * GROUP + lax.rem(lax.rem(me, GROUP) + k, GROUP)

    def other_group(k):
        return lax.rem(me + k * GROUP, n)

    barrier = pltpu.get_barrier_semaphore()
    partners = [halo_target(w) for w in range(neighbours)]
    partners += [group_mate(k) for k in range(1, GROUP)]
    partners += [other_group(k) for k in range(1, groups)]
    for partner in partners:
        pl.semaphore_signal(barrier, inc=1, device_id=(partner,), device_id_type=MESH)

    prev_copy = pltpu.make_async_copy(prev_hbm, prev, prev_sem)

    def tile_copy(c):
        piece = pl.ds(c * size, size)
        return pltpu.make_async_copy(tiles_hbm.at[piece], tiles.at[piece], tile_sem.at[c])

    for copy in entries[2:]:
        copy.start()

    def gather(step, half, which):
        base = ((step * 2 + half) * neighbours + which) * count
        for s in range(count):
            index = sends_ref[which, 0, s]
            if step == 0:
                outgoing[base + s] = (start_b if half else start_a)[index]
            else:
                outgoing[base + s] = own[step][half][index]

    def halo_copy(step, half, which):
        slot = (step * 2 + half) * neighbours + which
        return pltpu.make_async_remote_copy(
            src_ref=outgoing.at[pl.ds(slot * count, count)],
            dst_ref=ext[step][half].at[pl.ds(capacity + which * count, count)],
            send_sem=halo_send.at[step * 2 + half],
            recv_sem=halo_recv.at[step * 2 + half],
            device_id=(halo_target(which),),
            device_id_type=MESH,
        )

    def halo_whole(step, half):
        ghosts = neighbours * count
        return pltpu.make_async_remote_copy(
            src_ref=outgoing.at[pl.ds((step * 2 + half) * ghosts, ghosts)],
            dst_ref=ext[step][half].at[pl.ds(capacity, ghosts)],
            send_sem=halo_send.at[step * 2 + half],
            recv_sem=halo_recv.at[step * 2 + half],
            device_id=(halo_target(0),),
            device_id_type=MESH,
        )

    order = (4, 5, 2, 3, 0, 1)
    entries[0].wait()
    entries[1].wait()
    prev_copy.start()
    tile_copy(0).start()
    for which in order:
        gather(0, 0, which)
    pl.semaphore_wait(barrier, len(partners))
    for which in order:
        halo_copy(0, 0, which).start()
    entries[2].wait()
    for which in order:
        gather(0, 1, which)

    for copy in entries[3:]:
        copy.wait()
    live = live_ref[0]

    def mask(b):
        return jnp.where(b < live, 1.0, 0.0).astype(F32)

    def fill(b, carry):
        ext_a0[b] = (start_a[b].astype(F32) * mask(b)).astype(BF16)
        ext_b0[b] = (start_b[b].astype(F32) * mask(b)).astype(BF16)
        return carry

    lax.fori_loop(0, capacity, fill, 0, unroll=4)

    def within_copy(which, k):
        return pltpu.make_async_remote_copy(
            src_ref=mine.at[2 * which],
            dst_ref=within.at[which * (GROUP - 1) + k - 1],
            send_sem=sum_send.at[2 * which],
            recv_sem=sum_recv.at[2 * which],
            device_id=(group_mate(k),),
            device_id_type=MESH,
        )

    def across_copy(which, k):
        return pltpu.make_async_remote_copy(
            src_ref=mine.at[2 * which + 1],
            dst_ref=across.at[which * (groups - 1) + k - 1],
            send_sem=sum_send.at[2 * which + 1],
            recv_sem=sum_recv.at[2 * which + 1],
            device_id=(other_group(k),),
            device_id_type=MESH,
        )

    def sum_whole(which, landing):
        peers = landing.shape[0] // 2
        slot = 2 * which + (0 if landing is within else 1)
        return pltpu.make_async_remote_copy(
            src_ref=landing.at[pl.ds(which * peers, peers)],
            dst_ref=landing.at[pl.ds(which * peers, peers)],
            send_sem=sum_send.at[slot],
            recv_sem=sum_recv.at[slot],
            device_id=(group_mate(1),),
            device_id_type=MESH,
        )

    def sum_start(which, value):
        mine[2 * which] = value
        for k in range(1, GROUP):
            within_copy(which, k).start()

    def sum_middle(which):
        total = mine[2 * which]
        sum_whole(which, within).wait_recv()
        for k in range(1, GROUP):
            total += within[which * (GROUP - 1) + k - 1]
        mine[2 * which + 1] = total
        for k in range(1, groups):
            across_copy(which, k).start()

    def sum_end(which):
        total = mine[2 * which + 1]
        sum_whole(which, across).wait_recv()
        for k in range(1, groups):
            total += across[which * (groups - 1) + k - 1]
        return total

    prev_copy.wait()
    for c in range(1, CHUNKS):
        tile_copy(c).start()

    def prev_gram(pair, total):
        left, right = [], []
        for b in (2 * pair, 2 * pair + 1):
            high, low = split(prev[b] * mask(b))
            y_high[b, :32] = high
            y_low[b, :32] = low
            left.append(jnp.concatenate([high, low], axis=0))
            right.append(jnp.concatenate([high, high, low, low], axis=0))
        return total + rows_dot(
            jnp.concatenate(left, axis=1), jnp.concatenate(right, axis=1)
        )

    total = lax.fori_loop(0, capacity // 2, prev_gram, jnp.zeros((64, 128), F32), unroll=2)
    sum_start(0, pack(total[:32] + total[32:]))
    halo_whole(0, 0).wait_send()
    for which in order:
        halo_copy(0, 1, which).start()

    def product(step, half, b):
        vectors = ext[step][half]
        picked = jnp.concatenate([vectors[cols_ref[k, b]] for k in range(fan)], axis=1)
        return jnp.dot(picked, tiles[b], preferred_element_type=F32) * mask(b)

    c0, c1, c2, c3 = (coeff_ref[i] for i in range(4))

    def first_step(half, b):
        result = product(0, half, b)
        rounded = result.astype(BF16)
        first[half, b] = result
        own[1][half][b] = rounded
        ext[1][half][b] = rounded

    def second_step(half, b):
        before = ext[0][half][b].astype(F32)
        one = first[half, b]
        result = 2.0 * product(1, half, b) - before
        rounded = result.astype(BF16)
        own[2][half][b] = rounded
        ext[2][half][b] = rounded
        accum[half, b] = c0 * before + (c1 - c3) * one + c2 * result

    def third_step(half, b):
        rows = slice(32 + 16 * half, 48 + 16 * half)
        high, low = split(accum[half, b] + (2.0 * c3) * product(2, half, b))
        y_high[b, rows] = high
        y_low[b, rows] = low

    def await_halo(step, half):
        halo_whole(step, half).wait_recv()

    def loop(body, lower, upper):
        def one(b, carry):
            body(b)
            return carry

        lax.fori_loop(lower, upper, one, 0, unroll=BLOCKS)

    for half in range(2):
        await_halo(0, half)
        if half == 0:
            for c in range(CHUNKS):
                tile_copy(c).wait()
        loop(functools.partial(first_step, half), 0, capacity)
        for which in order:
            gather(1, half, which)
        if half == 0:
            halo_whole(0, 1).wait_send()
        for which in order:
            halo_copy(1, half, which).start()
        if half == 0:
            sum_middle(0)

    rows, lanes = iota(0), iota(1)
    gram = unpack(sum_end(0))
    matrix = jnp.where(lanes < 32, gram, jnp.where(lanes == rows + 64, 1.0, 0.0))
    matrix, diagonal = eliminate(matrix, True)
    middle = (lanes >= 32) & (lanes < 64)
    state_ref[:32] = jnp.where(middle, pltpu.roll(matrix / diagonal, 96, 1), 0.0)

    for half in range(2):
        await_halo(1, half)
        loop(functools.partial(second_step, half), 0, capacity)
        for which in order:
            gather(2, half, which)
            halo_copy(2, half, which).start()

    await_halo(2, 0)
    def third_group(half, group):
        for i in range(SPAN):
            third_step(half, group * SPAN + i)

    def filtered_gram(group, total):
        for i in range(0, SPAN, 2):
            left, right = [], []
            for b in (group * SPAN + i, group * SPAN + i + 1):
                left.append(jnp.concatenate([y_high[b, 32:64], y_low[b, 32:64]], axis=0))
                right.append(jnp.concatenate([y_high[b], y_low[b]], axis=0))
            total += rows_dot(
                jnp.concatenate(left, axis=1), jnp.concatenate(right, axis=1)
            )
        return total

    def last_group(group, total):
        total = filtered_gram(group - 1, total)
        third_group(1, group)
        return total

    loop(functools.partial(third_step, 0), 0, capacity)
    await_halo(2, 1)
    third_group(1, 0)
    total = lax.fori_loop(1, capacity // SPAN, last_group, jnp.zeros((64, 128), F32))
    total = filtered_gram(capacity // SPAN - 1, total)
    out_copies = [
        pltpu.make_async_copy(y_high, high_hbm, out_sem.at[0]),
        pltpu.make_async_copy(y_low, low_hbm, out_sem.at[1]),
    ]
    sum_start(1, pack(total[:32] + total[32:]))
    for copy in out_copies:
        copy.start()
    sum_middle(1)
    state_ref[32:] = unpack(sum_end(1))
    for copy in out_copies:
        copy.wait()
    for step in range(1, 3):
        for half in range(2):
            halo_whole(step, half).wait_send()
    for which in range(2):
        sum_whole(which, within).wait_send()
        sum_whole(which, across).wait_send()


def finish(
    scale, state_hbm, high_hbm, low_hbm, out_hbm, state, high, low, out,
    state_sem, in_sem, out_sem,
):
    size = high.shape[0] // PARTS
    pieces = [pl.ds(c * size, size) for c in range(PARTS)]
    reads = [
        [
            pltpu.make_async_copy(high_hbm.at[piece], high.at[piece], in_sem.at[0, c]),
            pltpu.make_async_copy(low_hbm.at[piece], low.at[piece], in_sem.at[1, c]),
        ]
        for c, piece in enumerate(pieces)
    ]
    writes = [
        pltpu.make_async_copy(out.at[piece], out_hbm.at[piece], out_sem.at[c])
        for c, piece in enumerate(pieces)
    ]
    state_copy = pltpu.make_async_copy(state_hbm, state, state_sem)
    state_copy.start()
    for pair in reads:
        for copy in pair:
            copy.start()
    state_copy.wait()
    factor = solve(scale, state[...])
    for c in range(PARTS):
        for copy in reads[c]:
            copy.wait()
        for b in range(c * size, (c + 1) * size, 2):
            stacked = [
                jnp.concatenate([high[i], high[i], low[i], low[i]], axis=0) for i in (b, b + 1)
            ]
            result = jnp.dot(
                factor, jnp.concatenate(stacked, axis=1), preferred_element_type=F32
            )
            out[b] = result[:, :128]
            out[b + 1] = result[:, 128:]
        writes[c].start()
    for copy in writes:
        copy.wait()


def shards(
    live_blocks, tile_columns, send_lists, tiles, filter_coeffs, start_block, previous_block
):
    n = lax.axis_size("rows")
    capacity, vectors, rows = start_block.shape
    fan = tile_columns.shape[1]
    _, neighbours, count = send_lists.shape
    groups = n // GROUP
    vmem = pl.BlockSpec(memory_space=pltpu.VMEM)
    hbm = pl.BlockSpec(memory_space=pl.ANY)
    half = vectors // 2
    field = pltpu.VMEM((capacity, half, rows), BF16)
    extended = pltpu.VMEM((capacity + neighbours * count, half, rows), BF16)
    wide = pltpu.VMEM((2, capacity, half, rows), F32)
    stacked = pltpu.VMEM((capacity, 2 * vectors, rows), BF16)
    scale = math.sqrt(capacity * n * rows)
    state, high, low = pl.pallas_call(
        functools.partial(kernel, n),
        out_shape=[jax.ShapeDtypeStruct((2 * vectors, 128), F32)]
        + [jax.ShapeDtypeStruct((capacity, 2 * vectors, rows), BF16)] * 2,
        in_specs=[hbm] * 7,
        out_specs=[vmem, hbm, hbm],
        scratch_shapes=[
            pltpu.SMEM(live_blocks.shape, jnp.int32),
            pltpu.SMEM((fan, capacity), jnp.int32),
            pltpu.SMEM((neighbours, 1, count), jnp.int32),
            pltpu.SMEM(filter_coeffs.shape, F32),
            field,
            field,
            pltpu.VMEM((capacity, fan * rows, rows), BF16),
            pltpu.VMEM((capacity, vectors, rows), F32),
            *[extended] * 6,
            *[field] * 4,
            pltpu.VMEM((6 * neighbours * count, half, rows), BF16),
            wide,
            wide,
            stacked,
            stacked,
            pltpu.VMEM((4, 16, 128), F32),
            pltpu.VMEM((2 * (GROUP - 1), 16, 128), F32),
            pltpu.VMEM((2 * (groups - 1), 16, 128), F32),
            pltpu.SemaphoreType.DMA((6,)),
            pltpu.SemaphoreType.DMA((CHUNKS,)),
            pltpu.SemaphoreType.DMA,
            pltpu.SemaphoreType.DMA((2,)),
            pltpu.SemaphoreType.DMA((6,)),
            pltpu.SemaphoreType.DMA((6,)),
            pltpu.SemaphoreType.DMA((4,)),
            pltpu.SemaphoreType.DMA((4,)),
        ],
        compiler_params=pltpu.CompilerParams(
            collective_id=0, has_side_effects=True, vmem_limit_bytes=64 * 1024 * 1024
        ),
        name="filtered_step",
    )(
        live_blocks,
        tile_columns.T,
        jnp.transpose(send_lists, (1, 0, 2)),
        filter_coeffs,
        start_block,
        tiles.reshape(capacity, fan * rows, rows),
        previous_block,
    )
    return pl.pallas_call(
        functools.partial(finish, scale),
        out_shape=jax.ShapeDtypeStruct((capacity, vectors, rows), F32),
        in_specs=[hbm, hbm, hbm],
        out_specs=hbm,
        scratch_shapes=[
            pltpu.VMEM((2 * vectors, 128), F32),
            stacked,
            stacked,
            pltpu.VMEM((capacity, vectors, rows), F32),
            pltpu.SemaphoreType.DMA,
            pltpu.SemaphoreType.DMA((2, PARTS)),
            pltpu.SemaphoreType.DMA((PARTS,)),
        ],
        compiler_params=pltpu.CompilerParams(vmem_limit_bytes=64 * 1024 * 1024),
        name="finish",
    )(state, high, low)


def solution(mesh):
    return jax.shard_map(
        shards,
        mesh=mesh,
        in_specs=(
            P("rows"),
            P("rows", None),
            P("rows", None, None),
            P("rows", None, None, None),
            P(),
            P("rows", None, None),
            P("rows", None, None),
        ),
        out_specs=P("rows", None, None),
        check_vma=False,
    )
```
